128 devices in a mesh: tile: 16 (over z, y_hi, core), spec: 8 (over y_lo, x).
Axes of the slice: x: 4, y: 4 (y_hi: 2, y_lo: 2; y = y_hi * 2 + y_lo), z: 4, core: 2. Of those that a mesh axis runs over, the one named last changes fastest.
Arguments:
- tracer: float32 [256, 8, 96, 1440], P('spec', None, 'tile'), may hold values from -6 to 6
- air_mass: float32 [8, 96, 1440], P('spec', 'tile'), may hold values from 2 to 4
- zonal_flux: float32 [8, 96, 1440], P('spec', 'tile'), may hold values from -1.6 to 1.6, as said below
- meridional_flux: float32 [8, 96, 1440], P('spec', 'tile'), may hold values from -0.15 to 0.15
- substeps: int32 [96], replicated, may hold values from 1 to 4, as said below
Outputs:
- tracer_out: float32 [256, 8, 96, 1440], P('spec', None, 'tile')
- mass_out: float32 [8, 96, 1440], P(None, 'tile')
The draws below stay inside these ranges and needn't reach their ends.
Inputs may be any that keep to these rules, and one draw needn't show every extreme that they name: `substeps`: the count of latitude row j is 1 + (j * 4) // 96 or one more, never over 4; the last row has 4. `zonal_flux`: each entry has magnitude at most 0.4 times its row's substep count, and two neighbouring entries of a row differ by at most 0.2 times that count.
All inputs are finite; a program needn't handle non-finite values.
Results may differ from the reference program's by a relative error of at most 0.0003.
Values sent between devices are 32-bit elements; how exact they have to be, the bound alone decides.
A program may use at most 320 MiB of HBM per device.

```python
import jax
import jax.numpy as jnp
from jax import lax

SPECIES = 256
NX = 1440
LEV = 8
MAX_SUB = 4
NY = 96


def ramp_counts(key):
    rows = jnp.arange(NY)
    base = rows * MAX_SUB // NY
    extra = jax.random.randint(jax.random.fold_in(key, 11), (NY,), 0, 3)
    return jnp.maximum(1 + base, jnp.minimum(MAX_SUB, base + extra)).astype(jnp.int32)


def draw_substeps(key, part):
    return ramp_counts(key)


def draw_zonal_flux(key, part):
    counts = ramp_counts(key)
    key = jax.random.fold_in(key, 5)
    row_key = jax.random.fold_in(key, 1)
    cell_key = jax.random.fold_in(key, 2)
    wind = jax.random.uniform(row_key, (LEV, NY, 1), jnp.float32, -0.3, 0.3)
    rough = jax.random.uniform(cell_key, (LEV, NY, NX), jnp.float32, -0.1, 0.1)
    speed = wind + rough
    return (speed * counts.astype(jnp.float32)[None, :, None]).astype(jnp.float32)


def steps_of(stream_key, shape, shards, least, high):
    def one(dim, parts):
        heights = jax.random.uniform(jax.random.fold_in(jax.random.fold_in(stream_key, 6), dim), (parts,), jnp.float32, least / len(shards), high / len(shards))
        return jnp.repeat(jnp.exp(heights), shape[dim] // parts).reshape((-1,) + (1,) * (len(shape) - dim - 1))

    level = one(*shards[0])
    for cut in shards[1:]:
        level = level * one(*cut)
    return level


def normal_values(key, dims, width, bound, split=(), held_as=jnp.bfloat16):
    values = width * jax.random.normal(key, dims, jnp.float32)
    if split:
        values = values * steps_of(key, dims, split, -0.22, 0.18)
    return jnp.clip(values, -bound, bound).astype(held_as)


def setup_inputs(seed: int = 0) -> dict:
    streams_of = jax.random.split(jax.random.key(seed), 6)
    return {
        "tracer": normal_values(streams_of[0], (SPECIES, LEV, NY, NX), 1.0, 6.0, ((0, 8), (2, 16)), jnp.float32),
        "air_mass": jnp.clip(2.0 + 2.0 * jax.random.uniform(streams_of[1], (LEV, NY, NX), jnp.float32) ** steps_of(streams_of[1], (LEV, NY, NX), ((0, 8), (1, 16)), -0.2, 0.2), 2.0, 4.0),
        "zonal_flux": draw_zonal_flux(jax.random.fold_in(streams_of[5], 71), 0),
        "meridional_flux": jnp.clip(jax.random.uniform(streams_of[3], (LEV, NY, NX), jnp.float32, -0.15, 0.15) * steps_of(streams_of[3], (LEV, NY, NX), ((0, 8), (1, 16)), -0.4, 0.0), -0.15, 0.15),
        "substeps": draw_substeps(jax.random.fold_in(streams_of[5], 71), 0),
    }


def limited(back, fore):
    size = jnp.minimum(jnp.minimum(2.0 * jnp.abs(back), 2.0 * jnp.abs(fore)), 0.5 * jnp.abs(back + fore))
    return jnp.where(back * fore > 0, jnp.sign(back) * size, 0.0)


def zonal_step(ratio, mass, flux):
    west = jnp.roll(ratio, 1, -1)
    slope = limited(ratio - west, jnp.roll(ratio, -1, -1) - ratio)
    west_mass = jnp.roll(mass, 1, -1)
    upwind = west + 0.5 * (1.0 - flux / west_mass) * jnp.roll(slope, 1, -1)
    downwind = ratio - 0.5 * (1.0 + flux / mass) * slope
    carried = flux * jnp.where(flux > 0, upwind, downwind)
    new_mass = mass + flux - jnp.roll(flux, -1, -1)
    new_ratio = (mass * ratio + carried - jnp.roll(carried, -1, -1)) / new_mass
    return new_ratio, new_mass


def zonal_sweep(ratio, mass, flux, counts, loops):
    shares = flux / counts.astype(jnp.float32)[:, None]

    def advance(step, carry):
        cur_ratio, cur_mass = carry
        new_ratio, new_mass = zonal_step(cur_ratio, cur_mass, shares)
        active = (step < counts)[:, None]
        return jnp.where(active, new_ratio, cur_ratio), jnp.where(active, new_mass, cur_mass)

    return lax.fori_loop(0, loops, advance, (ratio, mass))


def meridional_sweep(ext_ratio, ext_mass, ext_flux, first_row, total_rows):
    rows = ext_ratio.shape[2] - 4
    back = ext_ratio[:, :, 1:rows + 3] - ext_ratio[:, :, 0:rows + 2]
    fore = ext_ratio[:, :, 2:rows + 4] - ext_ratio[:, :, 1:rows + 3]
    slope = limited(back, fore)
    face_index = first_row + jnp.arange(rows + 1)
    valid = ((face_index > 0) & (face_index < total_rows))[:, None]
    flux = jnp.where(valid, ext_flux[:, 2:rows + 3], 0.0)
    upwind = ext_ratio[:, :, 1:rows + 2] + 0.5 * (1.0 - flux / ext_mass[:, 1:rows + 2]) * slope[:, :, 0:rows + 1]
    downwind = ext_ratio[:, :, 2:rows + 3] - 0.5 * (1.0 + flux / ext_mass[:, 2:rows + 3]) * slope[:, :, 1:rows + 2]
    carried = flux * jnp.where(flux > 0, upwind, downwind)
    centre_mass = ext_mass[:, 2:rows + 2]
    new_mass = centre_mass + flux[:, :rows] - flux[:, 1:]
    new_ratio = (centre_mass * ext_ratio[:, :, 2:rows + 2] + carried[:, :, :rows] - carried[:, :, 1:]) / new_mass
    return new_ratio, new_mass


def reference(tracer, air_mass, zonal_flux, meridional_flux, substeps):
    group_size = 8
    blocks = tracer.reshape(SPECIES // group_size, group_size, LEV, NY, NX)
    flux_ext = jnp.pad(meridional_flux, ((0, 0), (2, 2), (0, 0)), mode="edge")

    def one_block(block):
        zonal_ratio, zonal_mass = zonal_sweep(block, air_mass, zonal_flux, substeps, MAX_SUB)
        ratio_ext = jnp.pad(zonal_ratio, ((0, 0), (0, 0), (2, 2), (0, 0)), mode="edge")
        mass_ext = jnp.pad(zonal_mass, ((0, 0), (2, 2), (0, 0)), mode="edge")
        return meridional_sweep(ratio_ext, mass_ext, flux_ext, 0, NY)

    ratios, masses = lax.map(one_block, blocks)
    return ratios.reshape(SPECIES, LEV, NY, NX), masses[0]
```

```python
import jax
import jax.numpy as jnp
from jax import lax
from jax.experimental import pallas as pl
from jax.experimental.pallas import tpu as pltpu
from jax.sharding import PartitionSpec as P

MESH = pl.DeviceIdType.MESH
NX = 1440
WIDE = 1536
LANES = 128
LEVELS = 8
ROWS = 6
STEPS = 4
GROUP = 2


def widened(row):
    return jnp.concatenate([row, row[:, :48], row[:, NX - 48 :]], axis=1)


def east(value):
    return pltpu.roll(value, WIDE - 1, 1)


def west(value):
    return pltpu.roll(value, 1, 1)


def half_slope(back, fore):
    low = jnp.maximum(jnp.minimum(back, fore), 0.0)
    high = jnp.minimum(jnp.maximum(back, fore), 0.0)
    return jnp.maximum(jnp.minimum(0.25 * (back + fore), low), high)


def kernel(
    tiles,
    tracer,
    air,
    zonal,
    merid,
    substeps,
    out,
    mass_out,
    landed,
    swept,
    gathered,
    whole,
    coef,
    last_mass,
    from_south,
    from_north,
    edge_south,
    edge_north,
    got_south,
    got_north,
    faces,
    cells,
    load_sem,
    gather_send,
    gather_recv,
    send_north,
    send_south,
    recv_south,
    recv_north,
    edge_send,
    edge_recv,
):
    tile = lax.axis_index("tile")
    spec = lax.axis_index("spec")
    groups = tracer.shape[0] // GROUP
    has_south = tile > 0
    has_north = tile < tiles - 1

    def load(group):
        part = pl.ds(group * GROUP, GROUP)
        return pltpu.make_async_copy(tracer.at[part], landed.at[part], load_sem.at[group])

    def start_load(group, carry):
        load(group).start()
        return carry

    lax.fori_loop(0, groups, start_load, 0)

    barrier = pltpu.get_barrier_semaphore()
    for step in range(1, LEVELS):
        peer = lax.rem(spec + step, LEVELS)
        pl.semaphore_signal(barrier, inc=1, device_id=(tile, peer), device_id_type=MESH)

    @pl.when(has_south)
    def _():
        pl.semaphore_signal(barrier, inc=1, device_id=(tile - 1, spec), device_id_type=MESH)

    @pl.when(has_north)
    def _():
        pl.semaphore_signal(barrier, inc=1, device_id=(tile + 1, spec), device_id_type=MESH)

    greeted = LEVELS - 1 + has_south.astype(jnp.int32) + has_north.astype(jnp.int32)
    pl.semaphore_wait(barrier, greeted)

    sources = (air, zonal, merid)

    def give(index, step):
        peer = lax.rem(spec + step, LEVELS)
        return pltpu.make_async_remote_copy(
            src_ref=sources[index],
            dst_ref=gathered.at[index, spec],
            send_sem=gather_send.at[index, step],
            recv_sem=gather_recv.at[index, spec],
            device_id=(tile, peer),
            device_id_type=MESH,
        )

    for step in range(1, LEVELS):
        for index in range(3):
            give(index, step).start()
    for index in range(3):
        gathered[index, spec] = sources[index][...]
    for step in range(1, LEVELS):
        level = lax.rem(spec + LEVELS - step, LEVELS)
        for index in range(3):
            pltpu.make_async_remote_copy(
                src_ref=sources[index],
                dst_ref=gathered.at[index, level],
                send_sem=gather_send.at[index, step],
                recv_sem=gather_recv.at[index, level],
                device_id=(tile, level),
                device_id_type=MESH,
            ).wait()
    for index in range(3):
        for level in range(LEVELS):
            for row in range(ROWS):
                whole[index, row, level : level + 1, :] = gathered[index, level, row]

    first = tile * ROWS

    def prepare(row, carry):
        count = substeps[first + row]
        share = widened(whole[1, row]) / count.astype(jnp.float32)
        mass = widened(whole[0, row])
        for step in range(STEPS):
            flux = jnp.where(step < count, share, 0.0)
            inner = jnp.where(
                flux > 0, 1.0 - flux / west(mass), -1.0 - flux / mass
            )
            coef[row, step, 0] = flux
            coef[row, step, 1] = inner
            coef[row, step, 2] = mass
            mass = mass + flux - east(flux)
            coef[row, step, 3] = 1.0 / mass
        last_mass[row] = mass
        return carry

    lax.fori_loop(0, ROWS, prepare, 0)

    edge_north[0] = last_mass[ROWS - 1]
    edge_south[0] = last_mass[0]
    edge_south[1] = widened(whole[2, 0])

    def edge_up():
        return pltpu.make_async_remote_copy(
            src_ref=edge_north,
            dst_ref=got_south,
            send_sem=edge_send.at[0],
            recv_sem=edge_recv.at[0],
            device_id=(tile + 1, spec),
            device_id_type=MESH,
        )

    def edge_down():
        return pltpu.make_async_remote_copy(
            src_ref=edge_south,
            dst_ref=got_north,
            send_sem=edge_send.at[1],
            recv_sem=edge_recv.at[1],
            device_id=(tile - 1, spec),
            device_id_type=MESH,
        )

    pl.when(has_north)(lambda: edge_up().start())
    pl.when(has_south)(lambda: edge_down().start())

    def up(group):
        return pltpu.make_async_remote_copy(
            src_ref=swept.at[pl.ds(group * GROUP, GROUP), pl.ds(ROWS - 2, 2)],
            dst_ref=from_south.at[group],
            send_sem=send_north.at[group],
            recv_sem=recv_south.at[group],
            device_id=(tile + 1, spec),
            device_id_type=MESH,
        )

    def down(group):
        return pltpu.make_async_remote_copy(
            src_ref=swept.at[pl.ds(group * GROUP, GROUP), pl.ds(0, 2)],
            dst_ref=from_north.at[group],
            send_sem=send_south.at[group],
            recv_sem=recv_north.at[group],
            device_id=(tile - 1, spec),
            device_id_type=MESH,
        )

    def sweep_row(species, row):
        ratio = widened(landed[species, row])
        for step in range(STEPS):
            flux = coef[row, step, 0]
            fore = east(ratio) - ratio
            back = west(fore)
            slope = half_slope(back, fore)
            eastward = flux > 0
            value = jnp.where(eastward, ratio - back, ratio) + coef[row, step, 1] * jnp.where(
                eastward, west(slope), slope
            )
            carried = flux * value
            ratio = (coef[row, step, 2] * ratio + carried - east(carried)) * coef[row, step, 3]
        swept[species, row] = ratio

    def zonal_group(group, carry):
        load(group).wait()

        def one_row(row, inner):
            for species in range(GROUP):
                sweep_row(group * GROUP + species, row)
            return inner

        lax.fori_loop(0, ROWS, one_row, 0)
        pl.when(has_north)(lambda: up(group).start())
        pl.when(has_south)(lambda: down(group).start())
        return carry

    lax.fori_loop(0, groups, zonal_group, 0)

    @pl.when(has_south)
    def _():
        edge_down().wait_send()
        edge_up().wait_recv()

    @pl.when(has_north)
    def _():
        edge_up().wait_send()
        edge_down().wait_recv()

    @pl.when(jnp.logical_not(has_south))
    def _():
        got_south[0] = last_mass[0]

    @pl.when(jnp.logical_not(has_north))
    def _():
        got_north[0] = last_mass[ROWS - 1]
        got_north[1] = jnp.zeros((LEVELS, WIDE), jnp.float32)

    masses = [got_south[0]] + [last_mass[row] for row in range(ROWS)] + [got_north[0]]
    fluxes = [jnp.where(has_south, widened(whole[2, 0]), 0.0)]
    fluxes += [widened(whole[2, row]) for row in range(1, ROWS)] + [got_north[1]]
    for face in range(ROWS + 1):
        flux = fluxes[face]
        faces[face, 0] = flux
        faces[face, 1] = jnp.where(
            flux > 0, 1.0 - flux / masses[face], -1.0 - flux / masses[face + 1]
        )
    for row in range(ROWS):
        mass = masses[row + 1] + fluxes[row] - fluxes[row + 1]
        cells[row, 0] = masses[row + 1]
        cells[row, 1] = 1.0 / mass
        mass_out[row] = mass[:, :NX]

    def merid_part(group, species, start, width):
        lanes = pl.ds(start, width)
        own = group * GROUP + species
        rows = [from_south[group, species, k, :, lanes] for k in range(2)]
        rows += [swept[own, row, :, lanes] for row in range(ROWS)]
        rows += [from_north[group, species, k, :, lanes] for k in range(2)]
        diffs = [rows[k + 1] - rows[k] for k in range(ROWS + 3)]
        slopes = [half_slope(diffs[k], diffs[k + 1]) for k in range(ROWS + 2)]
        carried = []
        for face in range(ROWS + 1):
            flux = faces[face, 0, :, lanes]
            northward = flux > 0
            value = jnp.where(northward, rows[face + 1], rows[face + 2]) + faces[
                face, 1, :, lanes
            ] * jnp.where(northward, slopes[face], slopes[face + 1])
            carried.append(flux * value)
        for row in range(ROWS):
            out[own, row, :, lanes] = (
                cells[row, 0, :, lanes] * rows[row + 2] + carried[row] - carried[row + 1]
            ) * cells[row, 1, :, lanes]

    full = NX // LANES

    def merid_group(group, carry):
        @pl.when(has_south)
        def _():
            up(group).wait_recv()
            down(group).wait_send()

        @pl.when(has_north)
        def _():
            down(group).wait_recv()
            up(group).wait_send()

        for species in range(GROUP):

            @pl.when(jnp.logical_not(has_south))
            def _():
                for k in range(2):
                    from_south[group, species, k] = swept[group * GROUP + species, 0]

            @pl.when(jnp.logical_not(has_north))
            def _():
                for k in range(2):
                    from_north[group, species, k] = swept[group * GROUP + species, ROWS - 1]

        def block(index, inner):
            for species in range(GROUP):
                merid_part(group, species, pl.multiple_of(index * LANES, LANES), LANES)
            return inner

        lax.fori_loop(0, full, block, 0)
        for species in range(GROUP):
            merid_part(group, species, full * LANES, NX - full * LANES)
        return carry

    lax.fori_loop(0, groups, merid_group, 0)


def shards(tiles, tracer, air_mass, zonal_flux, meridional_flux, substeps):
    species = tracer.shape[0]
    groups = species // GROUP
    rows_first = [jnp.transpose(x, (1, 0, 2)) for x in (air_mass, zonal_flux, meridional_flux)]
    f32 = jnp.float32
    dma = pltpu.SemaphoreType.DMA

    def body(*refs):
        kernel(tiles, *refs)

    vmem = pl.BlockSpec(memory_space=pltpu.VMEM)
    ratios, masses = pl.pallas_call(
        body,
        out_shape=(
            jax.ShapeDtypeStruct((species, ROWS, LEVELS, NX), f32),
            jax.ShapeDtypeStruct((ROWS, LEVELS, NX), f32),
        ),
        in_specs=[pl.BlockSpec(memory_space=pl.ANY), vmem, vmem, vmem, pl.BlockSpec(memory_space=pltpu.SMEM)],
        out_specs=(vmem, vmem),
        scratch_shapes=[
            pltpu.VMEM((species, ROWS, LEVELS, NX), f32),
            pltpu.VMEM((species, ROWS, LEVELS, WIDE), f32),
            pltpu.VMEM((3, LEVELS, ROWS, 1, NX), f32),
            pltpu.VMEM((3, ROWS, LEVELS, NX), f32),
            pltpu.VMEM((ROWS, STEPS, 4, LEVELS, WIDE), f32),
            pltpu.VMEM((ROWS, LEVELS, WIDE), f32),
            pltpu.VMEM((groups, GROUP, 2, LEVELS, WIDE), f32),
            pltpu.VMEM((groups, GROUP, 2, LEVELS, WIDE), f32),
            pltpu.VMEM((2, LEVELS, WIDE), f32),
            pltpu.VMEM((1, LEVELS, WIDE), f32),
            pltpu.VMEM((1, LEVELS, WIDE), f32),
            pltpu.VMEM((2, LEVELS, WIDE), f32),
            pltpu.VMEM((ROWS + 1, 2, LEVELS, WIDE), f32),
            pltpu.VMEM((ROWS, 2, LEVELS, WIDE), f32),
            dma((groups,)),
            dma((3, LEVELS)),
            dma((3, LEVELS)),
            dma((groups,)),
            dma((groups,)),
            dma((groups,)),
            dma((groups,)),
            dma((2,)),
            dma((2,)),
        ],
        compiler_params=pltpu.CompilerParams(
            collective_id=0, has_side_effects=True, vmem_limit_bytes=58 * 2**20
        ),
        cost_estimate=pl.CostEstimate(flops=10**9, bytes_accessed=2 * 10**7, transcendentals=0),
    )(jnp.transpose(tracer, (0, 2, 1, 3)), *rows_first, substeps)
    return jnp.transpose(ratios, (0, 2, 1, 3)), jnp.transpose(masses, (1, 0, 2))


def solution(mesh):
    tiles = mesh.shape["tile"]

    def run(*args):
        return shards(tiles, *args)

    placed = (
        P("spec", None, "tile", None),
        P("spec", "tile", None),
        P("spec", "tile", None),
        P("spec", "tile", None),
        P(),
    )
    return jax.shard_map(
        run,
        mesh=mesh,
        in_specs=placed,
        out_specs=(P("spec", None, "tile", None), P(None, "tile", None)),
        check_vma=False,
    )
```

```python
import jax
import jax.numpy as jnp
from jax import lax
from jax.experimental import pallas as pl
from jax.experimental.pallas import tpu as pltpu
from jax.sharding import PartitionSpec as P

MESH = pl.DeviceIdType.MESH
NX = 1440
LANES = 128
COLS = 12
WIDE = COLS * LANES
LEVELS = 8
ROWS = 6
STEPS = 4
GROUP = 2
PACK = LANES // LEVELS
FIELD_ROWS = 24
FULL = NX // LANES


def east(value):
    return jnp.concatenate([value[1:], pltpu.roll(value[0], LANES - 1, 1)[None]], axis=0)


def west(value):
    return jnp.concatenate([pltpu.roll(value[COLS - 1], 1, 1)[None], value[: COLS - 1]], axis=0)


def half_slope(back, fore):
    low = jnp.maximum(jnp.minimum(back, fore), 0.0)
    high = jnp.minimum(jnp.maximum(back, fore), 0.0)
    return jnp.maximum(jnp.minimum(0.25 * (back + fore), low), high)


def wrap(turned):
    turned[NX : NX + COLS, :] = turned[0:COLS, :]
    turned[WIDE - COLS : WIDE, :] = turned[NX - COLS : NX, :]


def every(turned, col):
    return turned[pl.ds(col, LANES, stride=COLS), :]


def kernel(
    tiles,
    tracer,
    air,
    zonal,
    merid,
    substeps,
    out,
    mass_out,
    swept,
    turned,
    turned_more,
    back_turned,
    mine,
    gathered,
    levels,
    field,
    coef,
    last_mass,
    from_south,
    from_north,
    edge_south,
    edge_north,
    got_south,
    got_north,
    faces,
    cells,
    masses_new,
    load_sem,
    gather_send,
    gather_recv,
    send_north,
    send_south,
    recv_south,
    recv_north,
    edge_send,
    edge_recv,
):
    tile = lax.axis_index("tile")
    spec = lax.axis_index("spec")
    species = tracer.shape[0]
    groups = species // GROUP
    packs = species // PACK
    has_south = tile > 0
    has_north = tile < tiles - 1

    def load(pack, row):
        part = pl.ds(pack * PACK, PACK)
        return pltpu.make_async_copy(
            tracer.at[part, row], out.at[part, row], load_sem.at[pack * ROWS + row]
        )

    def start_load(index, carry):
        load(index // ROWS, index % ROWS).start()
        return carry

    lax.fori_loop(0, packs * ROWS, start_load, 0)

    half = LEVELS // 2
    partner = lax.rem(spec + half, LEVELS)
    side = (spec // half) * half
    peers = [side + lax.rem(spec + step, half) for step in range(1, half)]

    barrier = pltpu.get_barrier_semaphore()
    for peer in [partner] + peers:
        pl.semaphore_signal(barrier, inc=1, device_id=(tile, peer), device_id_type=MESH)

    @pl.when(has_south)
    def _():
        pl.semaphore_signal(barrier, inc=1, device_id=(tile - 1, spec), device_id_type=MESH)

    @pl.when(has_north)
    def _():
        pl.semaphore_signal(barrier, inc=1, device_id=(tile + 1, spec), device_id_type=MESH)

    mine[...] = jnp.zeros_like(mine)
    for index, source in enumerate((air, zonal, merid)):
        mine[index * ROWS : (index + 1) * ROWS, :] = source[:, 0, :]
    gathered[spec] = mine[...]
    for buffer in (turned, turned_more):
        buffer[NX:WIDE, :] = jnp.ones((WIDE - NX, LANES), jnp.float32)

    greeted = half + has_south.astype(jnp.int32) + has_north.astype(jnp.int32)
    pl.semaphore_wait(barrier, greeted)

    def give(source, level, peer, slot):
        return pltpu.make_async_remote_copy(
            src_ref=source,
            dst_ref=gathered.at[level],
            send_sem=gather_send.at[slot],
            recv_sem=gather_recv.at[level],
            device_id=(tile, peer),
            device_id_type=MESH,
        )

    to_partner = give(mine, spec, partner, 0)
    to_partner.start()
    own = [give(mine, spec, peer, 1 + k) for k, peer in enumerate(peers)]
    for copy in own:
        copy.start()

    def turn_in(pack, row):
        load(pack, row).wait()
        part = pl.ds(pack * PACK, PACK)
        for col in range(FULL):
            lanes = slice(col * LANES, (col + 1) * LANES)
            turned[lanes, :] = out[part, row, :, lanes].reshape(LANES, LANES).T
        rest = slice(FULL * LANES, NX)
        turned[rest, :] = out[part, row, :, rest].reshape(LANES, NX - FULL * LANES).T
        wrap(turned)
        for col in range(COLS):
            swept[part, row, col] = every(turned, col).T.reshape(PACK, LEVELS, LANES)

    def turn_pack(pack):
        def one(row, carry):
            turn_in(pack, row)
            return carry

        lax.fori_loop(0, ROWS, one, 0)

    turn_pack(0)
    pltpu.make_async_remote_copy(
        src_ref=mine,
        dst_ref=gathered.at[partner],
        send_sem=gather_send.at[0],
        recv_sem=gather_recv.at[partner],
        device_id=(tile, partner),
        device_id_type=MESH,
    ).wait()
    passed = [give(gathered.at[partner], partner, peer, half + k) for k, peer in enumerate(peers)]
    for copy in passed:
        copy.start()
    for pack in range(1, packs):
        turn_pack(pack)
    for copy in own + passed:
        copy.wait_send()
    for step in range(1, half):
        level = side + lax.rem(spec + half - step, half)
        for got in (level, lax.rem(level + half, LEVELS)):
            give(mine, got, peers[0], 0).wait_recv()

    more = LEVELS * FIELD_ROWS - LANES
    for col in range(COLS):
        lanes = slice(col * LANES, min((col + 1) * LANES, NX))
        width = lanes.stop - lanes.start
        block = gathered[:, :, lanes].reshape(LEVELS * FIELD_ROWS, width)
        turned[lanes, :] = block[:LANES].T
        turned_more[lanes, 0:more] = block[LANES:].T
    wrap(turned)
    wrap(turned_more)
    for col in range(COLS):
        levels[col, 0:LANES] = every(turned, col).T
        levels[col, LANES : LANES + more] = every(turned_more, col).T[:more]
        for index in range(3):
            for row in range(ROWS):
                field[index, row, col] = levels[
                    col, pl.ds(index * ROWS + row, LEVELS, stride=FIELD_ROWS), :
                ]

    first = tile * ROWS

    def prepare(row, carry):
        count = substeps[first + row]
        share = field[1, row] / count.astype(jnp.float32)
        mass = field[0, row]
        for step in range(STEPS):
            flux = jnp.where(step < count, share, 0.0)
            coef[row, step, 0] = flux
            coef[row, step, 1] = jnp.where(flux > 0, 1.0 - flux / west(mass), -1.0 - flux / mass)
            coef[row, step, 2] = mass
            mass = mass + flux - east(flux)
            coef[row, step, 3] = 1.0 / mass
        last_mass[row] = mass
        return carry

    lax.fori_loop(0, ROWS, prepare, 0)

    edge_north[0] = last_mass[ROWS - 1]
    edge_south[0] = last_mass[0]
    edge_south[1] = field[2, 0]

    def edge_up():
        return pltpu.make_async_remote_copy(
            src_ref=edge_north,
            dst_ref=got_south,
            send_sem=edge_send.at[0],
            recv_sem=edge_recv.at[0],
            device_id=(tile + 1, spec),
            device_id_type=MESH,
        )

    def edge_down():
        return pltpu.make_async_remote_copy(
            src_ref=edge_south,
            dst_ref=got_north,
            send_sem=edge_send.at[1],
            recv_sem=edge_recv.at[1],
            device_id=(tile - 1, spec),
            device_id_type=MESH,
        )

    pl.when(has_north)(lambda: edge_up().start())
    pl.when(has_south)(lambda: edge_down().start())

    def up(group):
        return pltpu.make_async_remote_copy(
            src_ref=swept.at[pl.ds(group * GROUP, GROUP), pl.ds(ROWS - 2, 2)],
            dst_ref=from_south.at[group],
            send_sem=send_north.at[group],
            recv_sem=recv_south.at[group],
            device_id=(tile + 1, spec),
            device_id_type=MESH,
        )

    def down(group):
        return pltpu.make_async_remote_copy(
            src_ref=swept.at[pl.ds(group * GROUP, GROUP), pl.ds(0, 2)],
            dst_ref=from_north.at[group],
            send_sem=send_south.at[group],
            recv_sem=recv_north.at[group],
            device_id=(tile - 1, spec),
            device_id_type=MESH,
        )

    def sweep_row(index, row):
        ratio = swept[index, row]
        for step in range(STEPS):
            flux = coef[row, step, 0]
            fore = east(ratio) - ratio
            slope = half_slope(west(fore), fore)
            eastward = flux > 0
            value = jnp.where(eastward, west(ratio), ratio) + coef[row, step, 1] * jnp.where(
                eastward, west(slope), slope
            )
            carried = flux * value
            ratio = (coef[row, step, 2] * ratio + carried - east(carried)) * coef[row, step, 3]
        swept[index, row] = ratio

    def zonal_group(group, carry):
        def one_row(row, inner):
            for k in range(GROUP):
                sweep_row(group * GROUP + k, row)
            return inner

        lax.fori_loop(0, ROWS, one_row, 0)
        pl.when(has_north)(lambda: up(group).start())
        pl.when(has_south)(lambda: down(group).start())
        return carry

    lax.fori_loop(0, groups, zonal_group, 0)

    @pl.when(has_south)
    def _():
        edge_down().wait_send()
        edge_up().wait_recv()

    @pl.when(has_north)
    def _():
        edge_up().wait_send()
        edge_down().wait_recv()

    @pl.when(jnp.logical_not(has_south))
    def _():
        got_south[0] = last_mass[0]

    @pl.when(jnp.logical_not(has_north))
    def _():
        got_north[0] = last_mass[ROWS - 1]
        got_north[1] = jnp.zeros((COLS, LEVELS, LANES), jnp.float32)

    def row_mass(row):
        if row < 0:
            return got_south[0]
        return last_mass[row] if row < ROWS else got_north[0]

    def face_flux(face):
        if face == 0:
            return jnp.where(has_south, field[2, 0], 0.0)
        return field[2, face] if face < ROWS else got_north[1]

    for face in range(ROWS + 1):
        flux = face_flux(face)
        faces[face, 0] = flux
        faces[face, 1] = jnp.where(
            flux > 0, 1.0 - flux / row_mass(face - 1), -1.0 - flux / row_mass(face)
        )
    for row in range(ROWS):
        mass = row_mass(row) + faces[row, 0] - faces[row + 1, 0]
        cells[row, 0] = row_mass(row)
        cells[row, 1] = 1.0 / mass
        masses_new[row] = mass
    masses_new[ROWS:] = jnp.zeros((PACK - ROWS, COLS, LEVELS, LANES), jnp.float32)

    def turn_out(read, write):
        for col in range(COLS):
            back_turned[pl.ds(col, LANES, stride=COLS), :] = read(col).reshape(LANES, LANES).T
        for col in range(COLS):
            lanes = slice(col * LANES, min((col + 1) * LANES, NX))
            width = lanes.stop - lanes.start
            write(lanes, back_turned[lanes, :].T.reshape(PACK, LEVELS, width))

    def write_mass(lanes, value):
        mass_out[:, :, lanes] = value[:ROWS]

    turn_out(lambda col: masses_new[:, col], write_mass)

    def merid_part(group, k, col):
        index = group * GROUP + k
        rows = [from_south[group, k, j, col] for j in range(2)]
        rows += [swept[index, row, col] for row in range(ROWS)]
        rows += [from_north[group, k, j, col] for j in range(2)]
        diffs = [rows[j + 1] - rows[j] for j in range(ROWS + 3)]
        slopes = [half_slope(diffs[j], diffs[j + 1]) for j in range(ROWS + 2)]
        carried = []
        for face in range(ROWS + 1):
            flux = faces[face, 0, col]
            northward = flux > 0
            value = jnp.where(northward, rows[face + 1], rows[face + 2]) + faces[
                face, 1, col
            ] * jnp.where(northward, slopes[face], slopes[face + 1])
            carried.append(flux * value)
        for row in range(ROWS):
            swept[index, row, col] = (
                cells[row, 0, col] * rows[row + 2] + carried[row] - carried[row + 1]
            ) * cells[row, 1, col]

    def merid_group(group, carry):
        @pl.when(has_south)
        def _():
            up(group).wait_recv()
            down(group).wait_send()

        @pl.when(has_north)
        def _():
            down(group).wait_recv()
            up(group).wait_send()

        for k in range(GROUP):

            @pl.when(jnp.logical_not(has_south))
            def _():
                for j in range(2):
                    from_south[group, k, j] = swept[group * GROUP + k, 0]

            @pl.when(jnp.logical_not(has_north))
            def _():
                for j in range(2):
                    from_north[group, k, j] = swept[group * GROUP + k, ROWS - 1]

        def block(col, inner):
            for k in range(GROUP):
                merid_part(group, k, col)
            return inner

        lax.fori_loop(0, COLS, block, 0)
        return carry

    def finish(pack, carry):
        each = PACK // GROUP
        lax.fori_loop(pack * each, (pack + 1) * each, merid_group, 0)
        part = pl.ds(pack * PACK, PACK)

        def one(row, inner):
            def write(lanes, value):
                out[part, row, :, lanes] = value

            turn_out(lambda col: swept[part, row, col], write)
            return inner

        lax.fori_loop(0, ROWS, one, 0)
        return carry

    lax.fori_loop(0, packs, finish, 0)


def shards(tiles, tracer, air_mass, zonal_flux, meridional_flux, substeps):
    species = tracer.shape[0]
    groups = species // GROUP
    rows_first = [jnp.transpose(x, (1, 0, 2)) for x in (air_mass, zonal_flux, meridional_flux)]
    f32 = jnp.float32
    dma = pltpu.SemaphoreType.DMA

    def body(*refs):
        kernel(tiles, *refs)

    def rows(*lead):
        return pltpu.VMEM((*lead, COLS, LEVELS, LANES), f32)

    vmem = pl.BlockSpec(memory_space=pltpu.VMEM)
    ratios, masses = pl.pallas_call(
        body,
        out_shape=(
            pltpu.VMEM((species, ROWS, LEVELS, NX), f32),
            pltpu.VMEM((ROWS, LEVELS, NX), f32),
        ),
        in_specs=[
            pl.BlockSpec(memory_space=pl.ANY),
            vmem,
            vmem,
            vmem,
            pl.BlockSpec(memory_space=pltpu.SMEM),
        ],
        out_specs=(vmem, vmem),
        scratch_shapes=[
            rows(species, ROWS),
            pltpu.VMEM((WIDE, LANES), f32),
            pltpu.VMEM((WIDE, LANES), f32),
            pltpu.VMEM((WIDE, LANES), f32),
            pltpu.VMEM((FIELD_ROWS, NX), f32),
            pltpu.VMEM((LEVELS, FIELD_ROWS, NX), f32),
            pltpu.VMEM((COLS, LEVELS * FIELD_ROWS, LANES), f32),
            rows(3, ROWS),
            rows(ROWS, STEPS, 4),
            rows(ROWS),
            rows(groups, GROUP, 2),
            rows(groups, GROUP, 2),
            rows(2),
            rows(1),
            rows(1),
            rows(2),
            rows(ROWS + 1, 2),
            rows(ROWS, 2),
            rows(PACK),
            dma((species // PACK * ROWS,)),
            dma((LEVELS,)),
            dma((LEVELS,)),
            dma((groups,)),
            dma((groups,)),
            dma((groups,)),
            dma((groups,)),
            dma((2,)),
            dma((2,)),
        ],
        compiler_params=pltpu.CompilerParams(
            collective_id=0, has_side_effects=True, vmem_limit_bytes=50 * 2**20
        ),
        cost_estimate=pl.CostEstimate(flops=10**9, bytes_accessed=2 * 10**7, transcendentals=0),
    )(jnp.transpose(tracer, (0, 2, 1, 3)), *rows_first, substeps)
    return jnp.transpose(ratios, (0, 2, 1, 3)), jnp.transpose(masses, (1, 0, 2))


def solution(mesh):
    tiles = mesh.shape["tile"]

    def run(*args):
        return shards(tiles, *args)

    placed = (
        P("spec", None, "tile", None),
        P("spec", "tile", None),
        P("spec", "tile", None),
        P("spec", "tile", None),
        P(),
    )
    return jax.shard_map(
        run,
        mesh=mesh,
        in_specs=placed,
        out_specs=(P("spec", None, "tile", None), P(None, "tile", None)),
        check_vma=False,
    )
```

```python
import jax
import jax.numpy as jnp
from jax import lax
from jax.experimental import pallas as pl
from jax.experimental.pallas import tpu as pltpu
from jax.sharding import PartitionSpec as P

MESH = pl.DeviceIdType.MESH
NX = 1440
LANES = 128
COLS = 12
WIDE = COLS * LANES
LEVELS = 8
ROWS = 6
STEPS = 4
GROUP = 8
PIECE = 2
EACH = GROUP // PIECE
PACK = LANES // LEVELS
FIRST_ROWS = 16
FULL = NX // LANES


def east(value):
    return jnp.concatenate([value[1:], pltpu.roll(value[0], LANES - 1, 1)[None]], axis=0)


def west(value):
    return jnp.concatenate([pltpu.roll(value[COLS - 1], 1, 1)[None], value[: COLS - 1]], axis=0)


def half_slope(back, fore):
    low = jnp.maximum(jnp.minimum(back, fore), 0.0)
    high = jnp.minimum(jnp.maximum(back, fore), 0.0)
    return jnp.maximum(jnp.minimum(0.25 * (back + fore), low), high)


def wrap(turned):
    turned[NX : NX + COLS, :] = turned[0:COLS, :]
    turned[WIDE - COLS : WIDE, :] = turned[NX - COLS : NX, :]


def every(turned, col):
    return turned[pl.ds(col, LANES, stride=COLS), :]


def kernel(
    tiles,
    tracer,
    air,
    zonal,
    merid,
    substeps,
    out,
    mass_out,
    swept,
    turned,
    turned_more,
    back_turned,
    mine,
    mine_more,
    gathered,
    gathered_more,
    levels,
    levels_more,
    field,
    coef,
    last_mass,
    raw,
    outer,
    inner,
    kept_flux,
    kept_slope,
    edge_outer,
    edge_inner,
    got_outer,
    got_inner,
    faces,
    cells,
    masses_new,
    load_sem,
    gather_send,
    gather_recv,
    more_send,
    more_recv,
    outer_send,
    outer_recv,
    inner_send,
    inner_recv,
    edge_send,
    edge_recv,
):
    tile = lax.axis_index("tile")
    spec = lax.axis_index("spec")
    species = tracer.shape[0]
    groups = species // GROUP
    packs = species // PACK
    odd = lax.rem(tile, 2)
    is_odd = odd == 1
    outer_tile = tile + 2 * odd - 1
    inner_tile = tile + 1 - 2 * odd
    has_outer = jnp.logical_and(tile > 0, tile < tiles - 1)

    def place(row):
        return row + odd * (ROWS - 1 - 2 * row)

    def load(pack, row):
        part = pl.ds(pack * PACK, PACK)
        return pltpu.make_async_copy(
            tracer.at[part, row], out.at[part, row], load_sem.at[pack * ROWS + row]
        )

    def start_load(index, carry):
        load(lax.rem(index, packs), place(index // packs)).start()
        return carry

    lax.fori_loop(0, packs * ROWS, start_load, 0)

    half = LEVELS // 2
    partner = lax.rem(spec + half, LEVELS)
    side = (spec // half) * half
    peers = [side + lax.rem(spec + step, half) for step in range(1, half)]

    barrier = pltpu.get_barrier_semaphore()
    for peer in [partner] + peers:
        pl.semaphore_signal(barrier, inc=1, device_id=(tile, peer), device_id_type=MESH)
    pl.semaphore_signal(barrier, inc=1, device_id=(inner_tile, spec), device_id_type=MESH)

    @pl.when(has_outer)
    def _():
        pl.semaphore_signal(barrier, inc=1, device_id=(outer_tile, spec), device_id_type=MESH)

    mine[2 * ROWS :, :] = jnp.zeros((FIRST_ROWS - 2 * ROWS, NX), jnp.float32)
    mine_more[ROWS:, :] = jnp.zeros((LEVELS - ROWS, NX), jnp.float32)
    for row in range(ROWS):
        mine[row : row + 1, :] = air[place(row)]
        mine[ROWS + row : ROWS + row + 1, :] = zonal[place(row)]
        mine_more[row : row + 1, :] = merid[place(row)]
    gathered[spec] = mine[...]
    gathered_more[spec] = mine_more[...]

    greeted = half + 1 + has_outer.astype(jnp.int32)
    pl.semaphore_wait(barrier, greeted)

    first_kind = (mine, gathered, gather_send, gather_recv)
    more_kind = (mine_more, gathered_more, more_send, more_recv)

    def give(kind, level, peer, slot, source=None):
        own, target, send, recv = kind
        return pltpu.make_async_remote_copy(
            src_ref=own if source is None else source,
            dst_ref=target.at[level],
            send_sem=send.at[slot],
            recv_sem=recv.at[level],
            device_id=(tile, peer),
            device_id_type=MESH,
        )

    def give_own(kind):
        give(kind, spec, partner, 0).start()
        for k, peer in enumerate(peers):
            give(kind, spec, peer, 1 + k).start()

    def pass_on(kind):
        give(kind, partner, partner, 0).wait()
        for k, peer in enumerate(peers):
            give(kind, partner, peer, half + k, kind[1].at[partner]).start()

    def settle(kind):
        for k, peer in enumerate(peers):
            give(kind, spec, peer, 1 + k).wait_send()
            give(kind, partner, peer, half + k, kind[1].at[partner]).wait_send()
        for step in range(1, half):
            level = side + lax.rem(spec + half - step, half)
            for got in (level, lax.rem(level + half, LEVELS)):
                give(kind, got, partner, 0).wait_recv()

    def across(piece):
        part = pl.ds(piece * PIECE, PIECE)
        return pltpu.make_async_remote_copy(
            src_ref=out.at[part, pl.ds(odd * (ROWS - 2), 2)],
            dst_ref=raw.at[part],
            send_sem=outer_send.at[piece],
            recv_sem=outer_recv.at[piece],
            device_id=(outer_tile, spec),
            device_id_type=MESH,
        )

    def send_across(piece, due=True):
        @pl.when(jnp.logical_and(has_outer, due))
        def _():
            across(piece).start()

    give_own(first_kind)
    for row in range(2):
        for pack in range(packs):
            load(pack, place(row)).wait()

    give_own(more_kind)
    pass_on(first_kind)
    pass_on(more_kind)

    for piece in range(3):
        send_across(piece)

    for buffer in (turned, turned_more):
        buffer[NX:WIDE, :] = jnp.ones((WIDE - NX, LANES), jnp.float32)

    def turn_in(read, write, count):
        wide = count * LEVELS
        for col in range(COLS):
            lanes = slice(col * LANES, min((col + 1) * LANES, NX))
            width = lanes.stop - lanes.start
            turned[lanes, 0:wide] = read(lanes).reshape(wide, width).T
        wrap(turned)
        for col in range(COLS):
            write(col, every(turned, col).T[:wide].reshape(count, LEVELS, LANES))

    def turn_own(pack, row):
        part = pl.ds(pack * PACK, PACK)

        @pl.when(row >= 2)
        def _():
            load(pack, place(row)).wait()


        def write(col, value):
            swept[part, row, col] = value

        turn_in(lambda lanes: out[part, place(row), :, lanes], write, PACK)

    def turn_one(index, carry):
        send_across(3 + index // ROWS, lax.rem(index, ROWS) == ROWS - 2)
        turn_own(index // ROWS, lax.rem(index, ROWS))
        return carry

    lax.fori_loop(0, packs * ROWS, turn_one, 0)
    settle(first_kind)

    def turn_fields(source, level_ref, rows):
        wide = LEVELS * rows
        for col in range(COLS):
            lanes = slice(col * LANES, min((col + 1) * LANES, NX))
            width = lanes.stop - lanes.start
            turned_more[lanes, 0:wide] = source[:, :, lanes].reshape(wide, width).T
        wrap(turned_more)
        for col in range(COLS):
            level_ref[col] = every(turned_more, col).T[:wide]

    turn_fields(gathered, levels, FIRST_ROWS)
    for col in range(COLS):
        for index in range(2):
            for row in range(ROWS):
                field[index, row, col] = levels[
                    col, pl.ds(index * ROWS + row, LEVELS, stride=FIRST_ROWS), :
                ]

    first = tile * ROWS

    def prepare(slot, place_of, mass, share):
        count = substeps[place_of]
        share = share / count.astype(jnp.float32)
        for step in range(STEPS):
            flux = jnp.where(step < count, share, 0.0)
            coef[slot, step, 0] = flux
            coef[slot, step, 1] = jnp.where(flux > 0, 1.0 - flux / west(mass), -1.0 - flux / mass)
            coef[slot, step, 2] = mass
            mass = mass + flux - east(flux)
            coef[slot, step, 3] = 1.0 / mass
        last_mass[slot] = mass

    def prepare_own(row, carry):
        prepare(row, first + place(row), field[0, row], field[1, row])
        return carry

    lax.fori_loop(0, ROWS, prepare_own, 0)

    def sweep(ref, group, row, slot):
        for k in range(GROUP):
            index = group * GROUP + k
            ratio = ref[index, row]
            for step in range(STEPS):
                flux = coef[slot, step, 0]
                fore = east(ratio) - ratio
                slope = half_slope(west(fore), fore)
                eastward = flux > 0
                value = jnp.where(eastward, west(ratio), ratio) + coef[slot, step, 1] * jnp.where(
                    eastward, west(slope), slope
                )
                carried = flux * value
                ratio = (coef[slot, step, 2] * ratio + carried - east(carried)) * coef[
                    slot, step, 3
                ]
            ref[index, row] = ratio

    def beside(group):
        part = pl.ds(group * GROUP, GROUP)
        return pltpu.make_async_remote_copy(
            src_ref=swept.at[part, pl.ds(ROWS - 2, 2)],
            dst_ref=inner.at[part],
            send_sem=inner_send.at[group],
            recv_sem=inner_recv.at[group],
            device_id=(inner_tile, spec),
            device_id_type=MESH,
        )

    send_across(5)

    def sweep_inner(group, carry):
        send_across(6 + group // 2, lax.rem(group, 2) == 0)

        def one(row, inside):
            sweep(swept, group, ROWS - 2 + row, ROWS - 2 + row)
            return inside

        lax.fori_loop(0, 2, one, 0)
        beside(group).start()
        return carry

    lax.fori_loop(0, groups, sweep_inner, 0)

    settle(more_kind)
    turn_fields(gathered_more, levels_more, LEVELS)
    for col in range(COLS):
        for row in range(ROWS):
            field[2, row, col] = levels_more[col, pl.ds(row, LEVELS, stride=LEVELS), :]

    for index in range(2):
        for row in range(2):
            edge_outer[2 * index + row] = field[index, row]
    edge_outer[4] = field[2, 0]
    edge_inner[0] = last_mass[ROWS - 1]
    edge_inner[1] = field[2, ROWS - 1]

    def edge(index):
        return pltpu.make_async_remote_copy(
            src_ref=(edge_outer, edge_inner)[index],
            dst_ref=(got_outer, got_inner)[index],
            send_sem=edge_send.at[index],
            recv_sem=edge_recv.at[index],
            device_id=((outer_tile, inner_tile)[index], spec),
            device_id_type=MESH,
        )

    edge(1).start()
    pl.when(has_outer)(lambda: edge(0).start())

    def sweep_rest(index, carry):
        send_across(8 + index // 4, lax.rem(index, 4) == 0)
        sweep(swept, lax.rem(index, groups), index // groups, index // groups)
        return carry

    lax.fori_loop(0, groups * (ROWS - 2), sweep_rest, 0)

    edge(1).wait()

    def row_mass(row):
        if row < 0:
            return last_mass[ROWS]
        return last_mass[row] if row < ROWS else got_inner[0]

    def own_flux(row):
        if row < 0:
            return got_outer[4]
        return field[2, row] if row < ROWS else got_inner[1]

    def make_face(face):
        flux = jnp.where(is_odd, -own_flux(face - 1), own_flux(face))
        if face == 0:
            flux = jnp.where(has_outer, flux, 0.0)
        faces[face, 0] = flux
        faces[face, 1] = jnp.where(
            flux > 0, 1.0 - flux / row_mass(face - 1), -1.0 - flux / row_mass(face)
        )

    def make_cell(row):
        mass = row_mass(row) + faces[row, 0] - faces[row + 1, 0]
        cells[row, 0] = row_mass(row)
        cells[row, 1] = 1.0 / mass
        masses_new[row] = mass

    for face in range(1, ROWS + 1):
        make_face(face)
    for row in range(1, ROWS):
        make_cell(row)
    masses_new[ROWS:] = jnp.zeros((PACK - ROWS, COLS, LEVELS, LANES), jnp.float32)

    def turn_out(read, write, count):
        wide = count * LEVELS
        for col in range(COLS):
            back_turned[pl.ds(col, LANES, stride=COLS), 0:wide] = read(col).reshape(wide, LANES).T
        for col in range(COLS):
            lanes = slice(col * LANES, min((col + 1) * LANES, NX))
            width = lanes.stop - lanes.start
            write(lanes, back_turned[lanes, :].T[:wide].reshape(count, LEVELS, width))

    def write_mass(lanes, value):
        for row in range(ROWS):
            mass_out[place(row), :, lanes] = value[row]

    def through(face, col, near, far, near_slope, far_slope):
        flux = faces[face, 0, col]
        onward = flux > 0
        value = jnp.where(onward, near, far) + faces[face, 1, col] * jnp.where(
            onward, near_slope, far_slope
        )
        return flux * value

    def renewed(row, col, ratio, enters, leaves):
        return (cells[row, 0, col] * ratio + enters - leaves) * cells[row, 1, col]

    def merid_far(index, col):
        rows = [swept[index, row, col] for row in range(ROWS)]
        rows += [inner[index, 1, col], inner[index, 0, col]]
        diffs = [rows[j + 1] - rows[j] for j in range(ROWS + 1)]
        slopes = [None] + [half_slope(diffs[j - 1], diffs[j]) for j in range(1, ROWS + 1)]
        carried = {
            face: through(
                face, col, rows[face - 1], rows[face], slopes[face - 1], slopes[face]
            )
            for face in range(2, ROWS + 1)
        }
        kept_flux[index, col] = carried[2]
        kept_slope[index, col] = slopes[1]
        for row in range(2, ROWS):
            swept[index, row, col] = renewed(row, col, rows[row], carried[row], carried[row + 1])

    def merid_near(index, col):
        rows = [outer[index, 1, col], outer[index, 0, col]]
        rows += [swept[index, row, col] for row in range(2)]
        diffs = [rows[j + 1] - rows[j] for j in range(3)]
        slopes = [half_slope(diffs[j], diffs[j + 1]) for j in range(2)]
        slopes.append(kept_slope[index, col])
        first_flux = through(0, col, rows[1], rows[2], slopes[0], slopes[1])
        second_flux = through(1, col, rows[2], rows[3], slopes[1], slopes[2])
        swept[index, 0, col] = renewed(0, col, rows[2], first_flux, second_flux)
        swept[index, 1, col] = renewed(1, col, rows[3], second_flux, kept_flux[index, col])

    def write_out(part, row):
        def write(lanes, value):
            out[part, place(row), :, lanes] = value

        return write

    def merid_all(group, work, pairs):
        def block(index, carry):
            col = lax.rem(index, COLS)
            for k in range(pairs):
                work(group * GROUP + (index // COLS) * pairs + k, col)
            return carry

        lax.fori_loop(0, COLS * (GROUP // pairs), block, 0)

    def far_group(group, carry):
        send_across(12 + group // 2, lax.rem(group, 2) == 0)
        beside(group).wait()
        merid_all(group, merid_far, 2)
        return carry

    lax.fori_loop(0, groups, far_group, 0)

    def far_out(index, carry):
        send_across(14 + index // 4, lax.rem(index, 4) == 0)
        part = pl.ds((index // (ROWS - 2)) * PACK, PACK)
        row = 2 + lax.rem(index, ROWS - 2)
        turn_out(lambda col: swept[part, row, col], write_out(part, row), PACK)
        return carry

    lax.fori_loop(0, packs * (ROWS - 2), far_out, 0)

    pl.when(has_outer)(lambda: edge(0).wait())

    @pl.when(jnp.logical_not(has_outer))
    def _():
        for row in range(2):
            got_outer[row] = field[0, row]
            got_outer[2 + row] = field[1, row]
        got_outer[4] = jnp.zeros((COLS, LEVELS, LANES), jnp.float32)

    def prepare_outer(row, carry):
        there = first + (1 - odd) * (-1 - row) + odd * (ROWS + row)
        there = jnp.where(has_outer, there, first + place(0))
        prepare(ROWS + row, there, got_outer[row], got_outer[2 + row])
        return carry

    lax.fori_loop(0, 2, prepare_outer, 0)

    make_face(0)
    make_cell(0)
    turn_out(lambda col: masses_new[:, col], write_mass, PACK)

    def near_row(row):
        return odd * row + (1 - odd) * (1 - row)

    def near_group(group, carry):
        part = pl.ds(group * GROUP, GROUP)

        @pl.when(has_outer)
        def _():
            def arrive(k, inside):
                across(group * EACH + k).wait()
                return inside

            lax.fori_loop(0, EACH, arrive, 0)

            def one(row, inside):
                def write(col, value):
                    outer[part, row, col] = value

                turn_in(lambda lanes: raw[part, near_row(row), :, lanes], write, GROUP)
                sweep(outer, group, row, ROWS + row)
                return inside

            lax.fori_loop(0, 2, one, 0)

        @pl.when(jnp.logical_not(has_outer))
        def _():
            def same(k, inside):
                for row in range(2):
                    outer[group * GROUP + k, row] = swept[group * GROUP + k, 0]
                return inside

            lax.fori_loop(0, GROUP, same, 0)

        merid_all(group, merid_near, 4)

        def back(row, inside):
            turn_out(lambda col: swept[part, row, col], write_out(part, row), GROUP)
            return inside

        lax.fori_loop(0, 2, back, 0)
        return carry

    lax.fori_loop(0, groups, near_group, 0)


def shards(tiles, tracer, air_mass, zonal_flux, meridional_flux, substeps):
    species = tracer.shape[0]
    groups = species // GROUP
    rows_first = [jnp.transpose(x, (1, 0, 2)) for x in (air_mass, zonal_flux, meridional_flux)]
    f32 = jnp.float32
    dma = pltpu.SemaphoreType.DMA

    def body(*refs):
        kernel(tiles, *refs)

    def rows(*lead):
        return pltpu.VMEM((*lead, COLS, LEVELS, LANES), f32)

    vmem = pl.BlockSpec(memory_space=pltpu.VMEM)
    ratios, masses = pl.pallas_call(
        body,
        out_shape=(
            pltpu.VMEM((species, ROWS, LEVELS, NX), f32),
            pltpu.VMEM((ROWS, LEVELS, NX), f32),
        ),
        in_specs=[
            pl.BlockSpec(memory_space=pl.ANY),
            vmem,
            vmem,
            vmem,
            pl.BlockSpec(memory_space=pltpu.SMEM),
        ],
        out_specs=(vmem, vmem),
        scratch_shapes=[
            rows(species, ROWS),
            pltpu.VMEM((WIDE, LANES), f32),
            pltpu.VMEM((WIDE, LANES), f32),
            pltpu.VMEM((WIDE, LANES), f32),
            pltpu.VMEM((FIRST_ROWS, NX), f32),
            pltpu.VMEM((LEVELS, NX), f32),
            pltpu.VMEM((LEVELS, FIRST_ROWS, NX), f32),
            pltpu.VMEM((LEVELS, LEVELS, NX), f32),
            pltpu.VMEM((COLS, LEVELS * FIRST_ROWS, LANES), f32),
            pltpu.VMEM((COLS, LEVELS * LEVELS, LANES), f32),
            rows(3, ROWS),
            rows(ROWS + 2, STEPS, 4),
            rows(ROWS + 2),
            pltpu.VMEM((species, 2, LEVELS, NX), f32),
            rows(species, 2),
            rows(species, 2),
            rows(species),
            rows(species),
            rows(5),
            rows(2),
            rows(5),
            rows(2),
            rows(ROWS + 1, 2),
            rows(ROWS, 2),
            rows(PACK),
            dma((species // PACK * ROWS,)),
            dma((LEVELS,)),
            dma((LEVELS,)),
            dma((LEVELS,)),
            dma((LEVELS,)),
            dma((species // PIECE,)),
            dma((species // PIECE,)),
            dma((groups,)),
            dma((groups,)),
            dma((2,)),
            dma((2,)),
        ],
        compiler_params=pltpu.CompilerParams(
            collective_id=0, has_side_effects=True, vmem_limit_bytes=50 * 2**20
        ),
        cost_estimate=pl.CostEstimate(flops=10**9, bytes_accessed=2 * 10**7, transcendentals=0),
    )(jnp.transpose(tracer, (0, 2, 1, 3)), *rows_first, substeps)
    return jnp.transpose(ratios, (0, 2, 1, 3)), jnp.transpose(masses, (1, 0, 2))


def solution(mesh):
    tiles = mesh.shape["tile"]

    def run(*args):
        return shards(tiles, *args)

    placed = (
        P("spec", None, "tile", None),
        P("spec", "tile", None),
        P("spec", "tile", None),
        P("spec", "tile", None),
        P(),
    )
    return jax.shard_map(
        run,
        mesh=mesh,
        in_specs=placed,
        out_specs=(P("spec", None, "tile", None), P(None, "tile", None)),
        check_vma=False,
    )
```

```python
import jax
import jax.numpy as jnp
from jax import lax
from jax.experimental import pallas as pl
from jax.experimental.pallas import tpu as pltpu
from jax.sharding import PartitionSpec as P

MESH = pl.DeviceIdType.MESH
NX = 1440
LANES = 128
COLS = 12
WIDE = COLS * LANES
LEVELS = 8
ROWS = 6
STEPS = 4
GROUP = 8
PIECE = 2
EACH = GROUP // PIECE
RAW_GROUPS = 2
RAW_PIECES = RAW_GROUPS * EACH
WHOLE = NX // LANES * LANES
REST = NX - WHOLE
SHARE = LANES // REST
USED = NX // COLS
SPARE = LANES - USED
SLOTS = USED // SPARE
ROW_SETS = PIECE * 2
DENSE = ROW_SETS * COLS * USED // LANES
PACK = LANES // LEVELS
FIRST_ROWS = 16
FULL = NX // LANES


def east(value):
    return jnp.concatenate([value[1:], pltpu.roll(value[0], LANES - 1, 1)[None]], axis=0)


def west(value):
    return jnp.concatenate([pltpu.roll(value[COLS - 1], 1, 1)[None], value[: COLS - 1]], axis=0)


def half_slope(back, fore):
    low = jnp.maximum(jnp.minimum(back, fore), 0.0)
    high = jnp.minimum(jnp.maximum(back, fore), 0.0)
    return jnp.maximum(jnp.minimum(0.25 * (back + fore), low), high)


def wrap(turned):
    turned[NX : NX + COLS, :] = turned[0:COLS, :]
    turned[WIDE - COLS : WIDE, :] = turned[NX - COLS : NX, :]


def every(turned, col):
    return turned[pl.ds(col, LANES, stride=COLS), :]


def kernel(
    tiles,
    tracer,
    air,
    zonal,
    merid,
    substeps,
    out,
    mass_out,
    swept,
    turned,
    turned_more,
    back_turned,
    mine,
    mine_more,
    gathered,
    gathered_more,
    levels,
    levels_more,
    field,
    coef,
    last_mass,
    raw,
    rests,
    got_rests,
    dense,
    got_dense,
    outer,
    inner,
    kept_flux,
    kept_slope,
    edge_outer,
    edge_inner,
    got_outer,
    got_inner,
    faces,
    cells,
    masses_new,
    load_sem,
    gather_send,
    gather_recv,
    more_send,
    more_recv,
    outer_send,
    outer_recv,
    inner_send,
    inner_recv,
    edge_send,
    edge_recv,
):
    tile = lax.axis_index("tile")
    spec = lax.axis_index("spec")
    species = tracer.shape[0]
    groups = species // GROUP
    packs = species // PACK
    odd = lax.rem(tile, 2)
    is_odd = odd == 1
    outer_tile = tile + 2 * odd - 1
    inner_tile = tile + 1 - 2 * odd
    has_outer = jnp.logical_and(tile > 0, tile < tiles - 1)

    def place(row):
        return row + odd * (ROWS - 1 - 2 * row)

    def load(pack, row):
        part = pl.ds(pack * PACK, PACK)
        return pltpu.make_async_copy(
            tracer.at[part, row], out.at[part, row], load_sem.at[pack * ROWS + row]
        )

    def start_load(index, carry):
        load(lax.rem(index, packs), place(index // packs)).start()
        return carry

    lax.fori_loop(0, packs * ROWS, start_load, 0)

    half = LEVELS // 2
    partner = lax.rem(spec + half, LEVELS)
    side = (spec // half) * half
    peers = [side + lax.rem(spec + step, half) for step in range(1, half)]

    barrier = pltpu.get_barrier_semaphore()
    for peer in [partner] + peers:
        pl.semaphore_signal(barrier, inc=1, device_id=(tile, peer), device_id_type=MESH)
    pl.semaphore_signal(barrier, inc=1, device_id=(inner_tile, spec), device_id_type=MESH)

    @pl.when(has_outer)
    def _():
        pl.semaphore_signal(barrier, inc=1, device_id=(outer_tile, spec), device_id_type=MESH)

    mine[2 * ROWS :, :] = jnp.zeros((FIRST_ROWS - 2 * ROWS, NX), jnp.float32)
    mine_more[ROWS:, :] = jnp.zeros((LEVELS - ROWS, NX), jnp.float32)
    for row in range(ROWS):
        mine[row : row + 1, :] = air[place(row)]
        mine[ROWS + row : ROWS + row + 1, :] = zonal[place(row)]
        mine_more[row : row + 1, :] = merid[place(row)]
    gathered[spec] = mine[...]
    gathered_more[spec] = mine_more[...]

    greeted = half + 1 + has_outer.astype(jnp.int32)
    pl.semaphore_wait(barrier, greeted)

    first_kind = (mine, gathered, gather_send, gather_recv)
    more_kind = (mine_more, gathered_more, more_send, more_recv)

    def give(kind, level, peer, slot, source=None):
        own, target, send, recv = kind
        return pltpu.make_async_remote_copy(
            src_ref=own if source is None else source,
            dst_ref=target.at[level],
            send_sem=send.at[slot],
            recv_sem=recv.at[level],
            device_id=(tile, peer),
            device_id_type=MESH,
        )

    def give_own(kind):
        give(kind, spec, partner, 0).start()
        for k, peer in enumerate(peers):
            give(kind, spec, peer, 1 + k).start()

    def pass_on(kind):
        give(kind, partner, partner, 0).wait()
        for k, peer in enumerate(peers):
            give(kind, partner, peer, half + k, kind[1].at[partner]).start()

    def settle(kind):
        for k, peer in enumerate(peers):
            give(kind, spec, peer, 1 + k).wait_send()
            give(kind, partner, peer, half + k, kind[1].at[partner]).wait_send()
        for step in range(1, half):
            level = side + lax.rem(spec + half - step, half)
            for got in (level, lax.rem(level + half, LEVELS)):
                give(kind, got, partner, 0).wait_recv()

    def across(piece, swept_already):
        part = pl.ds(piece * PIECE, PIECE)
        if swept_already:
            source, target = dense.at[piece - RAW_PIECES], got_dense.at[piece - RAW_PIECES]
        else:
            lanes = pl.ds(0, WHOLE)
            source = out.at[part, pl.ds(odd * (ROWS - 2), 2), :, lanes]
            target = raw.at[part]
        return pltpu.make_async_remote_copy(
            src_ref=source,
            dst_ref=target,
            send_sem=outer_send.at[piece],
            recv_sem=outer_recv.at[piece],
            device_id=(outer_tile, spec),
            device_id_type=MESH,
        )

    def rest_across():
        return pltpu.make_async_remote_copy(
            src_ref=rests,
            dst_ref=got_rests,
            send_sem=edge_send.at[2],
            recv_sem=edge_recv.at[2],
            device_id=(outer_tile, spec),
            device_id_type=MESH,
        )

    lane = lax.broadcasted_iota(jnp.int32, (LEVELS, LANES), 1)

    def spot(index):
        return index // (2 * COLS), (index // COLS) % 2, index % COLS

    def pack_piece(piece):
        for index in range(DENSE):
            k, row, col = spot(index)
            value = swept[piece * PIECE + k, row, col]
            k, row, col = spot(DENSE + index // SLOTS)
            moved = pltpu.roll(
                swept[piece * PIECE + k, row, col], USED - SPARE * (index % SLOTS), 1
            )
            dense[piece - RAW_PIECES, index] = jnp.where(lane < USED, value, moved)

    def unpack_piece(piece):
        for index in range(DENSE):
            k, row, col = spot(index)
            outer[piece * PIECE + k, row, col] = got_dense[piece - RAW_PIECES, index]
        for last in range(ROW_SETS * COLS - DENSE):
            value = got_dense[piece - RAW_PIECES, last * SLOTS + SLOTS - 1]
            value = pltpu.roll(value, SPARE * (SLOTS - 1) + LANES - USED, 1)
            for slot in range(SLOTS - 1):
                moved = pltpu.roll(
                    got_dense[piece - RAW_PIECES, last * SLOTS + slot],
                    SPARE * slot + LANES - USED,
                    1,
                )
                inside = jnp.logical_and(lane >= SPARE * slot, lane < SPARE * (slot + 1))
                value = jnp.where(inside, moved, value)
            k, row, col = spot(DENSE + last)
            outer[piece * PIECE + k, row, col] = value

    def send_across(piece, swept_already, due=True):
        @pl.when(jnp.logical_and(has_outer, due))
        def _():
            if swept_already:
                pack_piece(piece)
            across(piece, swept_already).start()

    give_own(first_kind)
    for row in range(2):
        for pack in range(packs):
            load(pack, place(row)).wait()

    for group in range(RAW_GROUPS):
        for row in range(2):
            for k in range(GROUP // SHARE):
                rests[group, row, k] = jnp.concatenate(
                    [
                        out[
                            group * GROUP + j * (GROUP // SHARE) + k,
                            odd * (ROWS - 2) + row,
                            :,
                            WHOLE:NX,
                        ]
                        for j in range(SHARE)
                    ],
                    axis=1,
                )

    give_own(more_kind)
    for piece in range(1):
        send_across(piece, False)
    pass_on(first_kind)
    pass_on(more_kind)

    for piece in range(1, 3):
        send_across(piece, False)
    pl.when(has_outer)(lambda: rest_across().start())

    for buffer in (turned, turned_more):
        buffer[NX:WIDE, :] = jnp.ones((WIDE - NX, LANES), jnp.float32)

    def turn_in(read, write, count, rest=None):
        wide = count * LEVELS
        for col in range(COLS if rest is None else FULL):
            lanes = slice(col * LANES, min((col + 1) * LANES, NX))
            width = lanes.stop - lanes.start
            turned[lanes, 0:wide] = read(lanes).reshape(wide, width).T
        if rest is not None:
            few = wide // SHARE
            block = rest.reshape(few, LANES).T
            for j in range(SHARE):
                turned[WHOLE:NX, j * few : (j + 1) * few] = block[j * REST : (j + 1) * REST]
        wrap(turned)
        for col in range(COLS):
            write(col, every(turned, col).T[:wide].reshape(count, LEVELS, LANES))

    def turn_own(pack, row):
        part = pl.ds(pack * PACK, PACK)

        @pl.when(row >= 2)
        def _():
            load(pack, place(row)).wait()


        def write(col, value):
            swept[part, row, col] = value

        turn_in(lambda lanes: out[part, place(row), :, lanes], write, PACK)

    def turn_one(index, carry):
        send_across(3, False, index == packs * ROWS - 2)
        turn_own(index // ROWS, lax.rem(index, ROWS))
        return carry

    lax.fori_loop(0, packs * ROWS, turn_one, 0)
    settle(first_kind)

    def turn_fields(source, level_ref, rows):
        wide = LEVELS * rows
        for col in range(COLS):
            lanes = slice(col * LANES, min((col + 1) * LANES, NX))
            width = lanes.stop - lanes.start
            turned_more[lanes, 0:wide] = source[:, :, lanes].reshape(wide, width).T
        wrap(turned_more)
        for col in range(COLS):
            level_ref[col] = every(turned_more, col).T[:wide]

    turn_fields(gathered, levels, FIRST_ROWS)
    for col in range(COLS):
        for index in range(2):
            for row in range(ROWS):
                field[index, row, col] = levels[
                    col, pl.ds(index * ROWS + row, LEVELS, stride=FIRST_ROWS), :
                ]

    first = tile * ROWS

    def prepare(slot, place_of, mass, share):
        count = substeps[place_of]
        share = share / count.astype(jnp.float32)
        for step in range(STEPS):
            flux = jnp.where(step < count, share, 0.0)
            coef[slot, step, 0] = flux
            coef[slot, step, 1] = jnp.where(flux > 0, 1.0 - flux / west(mass), -1.0 - flux / mass)
            coef[slot, step, 2] = mass
            mass = mass + flux - east(flux)
            coef[slot, step, 3] = 1.0 / mass
        last_mass[slot] = mass

    def prepare_own(row, carry):
        prepare(row, first + place(row), field[0, row], field[1, row])
        return carry

    lax.fori_loop(0, ROWS, prepare_own, 0)

    def sweep(ref, group, row, slot):
        for k in range(GROUP):
            index = group * GROUP + k
            ratio = ref[index, row]
            for step in range(STEPS):
                flux = coef[slot, step, 0]
                fore = east(ratio) - ratio
                slope = half_slope(west(fore), fore)
                eastward = flux > 0
                value = jnp.where(eastward, west(ratio), ratio) + coef[slot, step, 1] * jnp.where(
                    eastward, west(slope), slope
                )
                carried = flux * value
                ratio = (coef[slot, step, 2] * ratio + carried - east(carried)) * coef[
                    slot, step, 3
                ]
            ref[index, row] = ratio

    def beside(group):
        part = pl.ds(group * GROUP, GROUP)
        return pltpu.make_async_remote_copy(
            src_ref=swept.at[part, pl.ds(ROWS - 2, 2)],
            dst_ref=inner.at[part],
            send_sem=inner_send.at[group],
            recv_sem=inner_recv.at[group],
            device_id=(inner_tile, spec),
            device_id_type=MESH,
        )

    send_across(4, False)

    def sweep_early(index, carry):
        row = lax.rem(index, 2)
        sweep(swept, RAW_GROUPS + index // 2, row, row)
        return carry

    lax.fori_loop(0, 2 * (groups - RAW_GROUPS), sweep_early, 0)

    def sweep_inner(group, carry):
        send_across(5 + group // 2, False, lax.rem(group, 2) == 0)

        def one(row, inside):
            sweep(swept, group, ROWS - 2 + row, ROWS - 2 + row)
            return inside

        lax.fori_loop(0, 2, one, 0)
        beside(group).start()
        return carry

    lax.fori_loop(0, groups, sweep_inner, 0)

    settle(more_kind)
    turn_fields(gathered_more, levels_more, LEVELS)
    for col in range(COLS):
        for row in range(ROWS):
            field[2, row, col] = levels_more[col, pl.ds(row, LEVELS, stride=LEVELS), :]

    for index in range(2):
        for row in range(2):
            edge_outer[2 * index + row] = field[index, row]
    edge_outer[4] = field[2, 0]
    edge_inner[0] = last_mass[ROWS - 1]
    edge_inner[1] = field[2, ROWS - 1]

    def edge(index):
        return pltpu.make_async_remote_copy(
            src_ref=(edge_outer, edge_inner)[index],
            dst_ref=(got_outer, got_inner)[index],
            send_sem=edge_send.at[index],
            recv_sem=edge_recv.at[index],
            device_id=((outer_tile, inner_tile)[index], spec),
            device_id_type=MESH,
        )

    edge(1).start()
    pl.when(has_outer)(lambda: edge(0).start())

    send_across(7, False)

    def sweep_middle(index, carry):
        send_across(RAW_PIECES + index // 4, True, lax.rem(index, 4) == 0)
        row = 2 + index // groups
        sweep(swept, lax.rem(index, groups), row, row)
        return carry

    lax.fori_loop(0, groups * (ROWS - 4), sweep_middle, 0)

    def sweep_late(index, carry):
        row = lax.rem(index, 2)
        sweep(swept, index // 2, row, row)
        return carry

    lax.fori_loop(0, 2 * RAW_GROUPS, sweep_late, 0)

    edge(1).wait()

    def row_mass(row):
        if row < 0:
            return last_mass[ROWS]
        return last_mass[row] if row < ROWS else got_inner[0]

    def own_flux(row):
        if row < 0:
            return got_outer[4]
        return field[2, row] if row < ROWS else got_inner[1]

    def make_face(face):
        flux = jnp.where(is_odd, -own_flux(face - 1), own_flux(face))
        if face == 0:
            flux = jnp.where(has_outer, flux, 0.0)
        faces[face, 0] = flux
        faces[face, 1] = jnp.where(
            flux > 0, 1.0 - flux / row_mass(face - 1), -1.0 - flux / row_mass(face)
        )

    def make_cell(row):
        mass = row_mass(row) + faces[row, 0] - faces[row + 1, 0]
        cells[row, 0] = row_mass(row)
        cells[row, 1] = 1.0 / mass
        masses_new[row] = mass

    for face in range(1, ROWS + 1):
        make_face(face)
    for row in range(1, ROWS):
        make_cell(row)
    masses_new[ROWS:] = jnp.zeros((PACK - ROWS, COLS, LEVELS, LANES), jnp.float32)

    def turn_out(read, write, count):
        wide = count * LEVELS
        for col in range(COLS):
            back_turned[pl.ds(col, LANES, stride=COLS), 0:wide] = read(col).reshape(wide, LANES).T
        for col in range(COLS):
            lanes = slice(col * LANES, min((col + 1) * LANES, NX))
            width = lanes.stop - lanes.start
            write(lanes, back_turned[lanes, :].T[:wide].reshape(count, LEVELS, width))

    def write_mass(lanes, value):
        for row in range(ROWS):
            mass_out[place(row), :, lanes] = value[row]

    def through(face, col, near, far, near_slope, far_slope):
        flux = faces[face, 0, col]
        onward = flux > 0
        value = jnp.where(onward, near, far) + faces[face, 1, col] * jnp.where(
            onward, near_slope, far_slope
        )
        return flux * value

    def renewed(row, col, ratio, enters, leaves):
        return (cells[row, 0, col] * ratio + enters - leaves) * cells[row, 1, col]

    def merid_far(index, col):
        rows = [swept[index, row, col] for row in range(ROWS)]
        rows += [inner[index, 1, col], inner[index, 0, col]]
        diffs = [rows[j + 1] - rows[j] for j in range(ROWS + 1)]
        slopes = [None] + [half_slope(diffs[j - 1], diffs[j]) for j in range(1, ROWS + 1)]
        carried = {
            face: through(
                face, col, rows[face - 1], rows[face], slopes[face - 1], slopes[face]
            )
            for face in range(2, ROWS + 1)
        }
        kept_flux[index, col] = carried[2]
        kept_slope[index, col] = slopes[1]
        for row in range(2, ROWS):
            swept[index, row, col] = renewed(row, col, rows[row], carried[row], carried[row + 1])

    def merid_near(index, col):
        rows = [outer[index, 1, col], outer[index, 0, col]]
        rows += [swept[index, row, col] for row in range(2)]
        diffs = [rows[j + 1] - rows[j] for j in range(3)]
        slopes = [half_slope(diffs[j], diffs[j + 1]) for j in range(2)]
        slopes.append(kept_slope[index, col])
        first_flux = through(0, col, rows[1], rows[2], slopes[0], slopes[1])
        second_flux = through(1, col, rows[2], rows[3], slopes[1], slopes[2])
        swept[index, 0, col] = renewed(0, col, rows[2], first_flux, second_flux)
        swept[index, 1, col] = renewed(1, col, rows[3], second_flux, kept_flux[index, col])

    def write_out(part, row):
        def write(lanes, value):
            out[part, place(row), :, lanes] = value

        return write

    def merid_all(group, work, pairs):
        def block(index, carry):
            col = lax.rem(index, COLS)
            for k in range(pairs):
                work(group * GROUP + (index // COLS) * pairs + k, col)
            return carry

        lax.fori_loop(0, COLS * (GROUP // pairs), block, 0)

    def far_group(group, carry):
        send_across(10 + group // 2, True, lax.rem(group, 2) == 0)
        beside(group).wait()
        merid_all(group, merid_far, 2)
        return carry

    lax.fori_loop(0, groups, far_group, 0)

    def far_out(index, carry):
        send_across(12 + index // 4, True, lax.rem(index, 4) == 0)
        part = pl.ds((index // (ROWS - 2)) * PACK, PACK)
        row = 2 + lax.rem(index, ROWS - 2)
        turn_out(lambda col: swept[part, row, col], write_out(part, row), PACK)
        return carry

    lax.fori_loop(0, packs * (ROWS - 2), far_out, 0)
    for piece in (14, 15):
        send_across(piece, True)


    @pl.when(has_outer)
    def _():
        edge(0).wait()
        rest_across().wait()

    @pl.when(jnp.logical_not(has_outer))
    def _():
        for row in range(2):
            got_outer[row] = field[0, row]
            got_outer[2 + row] = field[1, row]
        got_outer[4] = jnp.zeros((COLS, LEVELS, LANES), jnp.float32)

    def prepare_outer(row, carry):
        there = first + (1 - odd) * (-1 - row) + odd * (ROWS + row)
        there = jnp.where(has_outer, there, first + place(0))
        prepare(ROWS + row, there, got_outer[row], got_outer[2 + row])
        return carry

    lax.fori_loop(0, 2, prepare_outer, 0)

    make_face(0)
    make_cell(0)
    turn_out(lambda col: masses_new[:, col], write_mass, PACK)

    def near_row(row):
        return odd * row + (1 - odd) * (1 - row)

    def near_group(group, swept_already):
        part = pl.ds(group * GROUP, GROUP)

        @pl.when(has_outer)
        def _():
            def arrive(k, inside):
                across(group * EACH + k, swept_already).wait()
                if swept_already:
                    unpack_piece(group * EACH + k)
                return inside

            lax.fori_loop(0, EACH, arrive, 0)

            def one(row, inside):
                def write(col, value):
                    outer[part, row, col] = value

                turn_in(
                    lambda lanes: raw[part, near_row(row), :, lanes],
                    write,
                    GROUP,
                    got_rests[group, near_row(row)],
                )
                sweep(outer, group, row, ROWS + row)
                return inside

            if not swept_already:
                lax.fori_loop(0, 2, one, 0)

        @pl.when(jnp.logical_not(has_outer))
        def _():
            def same(k, inside):
                for row in range(2):
                    outer[group * GROUP + k, row] = swept[group * GROUP + k, 0]
                return inside

            lax.fori_loop(0, GROUP, same, 0)

        merid_all(group, merid_near, 4)

        def back(row, inside):
            turn_out(lambda col: swept[part, row, col], write_out(part, row), GROUP)
            return inside

        lax.fori_loop(0, 2, back, 0)

    def near_raw(group, carry):
        near_group(group, False)
        return carry

    def near_swept(group, carry):
        near_group(group, True)
        return carry

    lax.fori_loop(0, RAW_GROUPS, near_raw, 0)
    lax.fori_loop(RAW_GROUPS, groups, near_swept, 0)


def shards(tiles, tracer, air_mass, zonal_flux, meridional_flux, substeps):
    species = tracer.shape[0]
    groups = species // GROUP
    rows_first = [jnp.transpose(x, (1, 0, 2)) for x in (air_mass, zonal_flux, meridional_flux)]
    f32 = jnp.float32
    dma = pltpu.SemaphoreType.DMA

    def body(*refs):
        kernel(tiles, *refs)

    def rows(*lead):
        return pltpu.VMEM((*lead, COLS, LEVELS, LANES), f32)

    vmem = pl.BlockSpec(memory_space=pltpu.VMEM)
    ratios, masses = pl.pallas_call(
        body,
        out_shape=(
            pltpu.VMEM((species, ROWS, LEVELS, NX), f32),
            pltpu.VMEM((ROWS, LEVELS, NX), f32),
        ),
        in_specs=[
            pl.BlockSpec(memory_space=pl.ANY),
            vmem,
            vmem,
            vmem,
            pl.BlockSpec(memory_space=pltpu.SMEM),
        ],
        out_specs=(vmem, vmem),
        scratch_shapes=[
            rows(species, ROWS),
            pltpu.VMEM((WIDE, LANES), f32),
            pltpu.VMEM((WIDE, LANES), f32),
            pltpu.VMEM((WIDE, LANES), f32),
            pltpu.VMEM((FIRST_ROWS, NX), f32),
            pltpu.VMEM((LEVELS, NX), f32),
            pltpu.VMEM((LEVELS, FIRST_ROWS, NX), f32),
            pltpu.VMEM((LEVELS, LEVELS, NX), f32),
            pltpu.VMEM((COLS, LEVELS * FIRST_ROWS, LANES), f32),
            pltpu.VMEM((COLS, LEVELS * LEVELS, LANES), f32),
            rows(3, ROWS),
            rows(ROWS + 2, STEPS, 4),
            rows(ROWS + 2),
            pltpu.VMEM((RAW_GROUPS * GROUP, 2, LEVELS, WHOLE), f32),
            pltpu.VMEM((RAW_GROUPS, 2, GROUP // SHARE, LEVELS, LANES), f32),
            pltpu.VMEM((RAW_GROUPS, 2, GROUP // SHARE, LEVELS, LANES), f32),
            pltpu.VMEM((species // PIECE - RAW_PIECES, DENSE, LEVELS, LANES), f32),
            pltpu.VMEM((species // PIECE - RAW_PIECES, DENSE, LEVELS, LANES), f32),
            rows(species, 2),
            rows(species, 2),
            rows(species),
            rows(species),
            rows(5),
            rows(2),
            rows(5),
            rows(2),
            rows(ROWS + 1, 2),
            rows(ROWS, 2),
            rows(PACK),
            dma((species // PACK * ROWS,)),
            dma((LEVELS,)),
            dma((LEVELS,)),
            dma((LEVELS,)),
            dma((LEVELS,)),
            dma((species // PIECE,)),
            dma((species // PIECE,)),
            dma((groups,)),
            dma((groups,)),
            dma((3,)),
            dma((3,)),
        ],
        compiler_params=pltpu.CompilerParams(
            collective_id=0, has_side_effects=True, vmem_limit_bytes=50 * 2**20
        ),
        cost_estimate=pl.CostEstimate(flops=10**9, bytes_accessed=2 * 10**7, transcendentals=0),
    )(jnp.transpose(tracer, (0, 2, 1, 3)), *rows_first, substeps)
    return jnp.transpose(ratios, (0, 2, 1, 3)), jnp.transpose(masses, (1, 0, 2))


def solution(mesh):
    tiles = mesh.shape["tile"]

    def run(*args):
        return shards(tiles, *args)

    placed = (
        P("spec", None, "tile", None),
        P("spec", "tile", None),
        P("spec", "tile", None),
        P("spec", "tile", None),
        P(),
    )
    return jax.shard_map(
        run,
        mesh=mesh,
        in_specs=placed,
        out_specs=(P("spec", None, "tile", None), P(None, "tile", None)),
        check_vma=False,
    )
```

```python
import jax
import jax.numpy as jnp
from jax import lax
from jax.experimental import pallas as pl
from jax.experimental.pallas import tpu as pltpu
from jax.sharding import PartitionSpec as P

MESH = pl.DeviceIdType.MESH
NX = 1440
LANES = 128
COLS = 12
WIDE = COLS * LANES
LEVELS = 8
ROWS = 6
STEPS = 4
GROUP = 8
PIECE = 2
EACH = GROUP // PIECE
RAW_GROUPS = 2
RAW_PIECES = RAW_GROUPS * EACH
WHOLE = NX // LANES * LANES
REST = NX - WHOLE
SHARE = LANES // REST
USED = NX // COLS
SPARE = LANES - USED
SLOTS = USED // SPARE
COPIES = 4
ROW_SETS = PIECE * 2
DENSE = ROW_SETS * COLS * USED // LANES
PACK = LANES // LEVELS
FIRST_ROWS = 16
FULL = NX // LANES


def east(value):
    return jnp.concatenate([value[1:], pltpu.roll(value[0], LANES - 1, 1)[None]], axis=0)


def west(value):
    return jnp.concatenate([pltpu.roll(value[COLS - 1], 1, 1)[None], value[: COLS - 1]], axis=0)


def half_slope(back, fore):
    low = jnp.maximum(jnp.minimum(back, fore), 0.0)
    high = jnp.minimum(jnp.maximum(back, fore), 0.0)
    return jnp.maximum(jnp.minimum(0.25 * (back + fore), low), high)


def wrap(turned):
    turned[NX : NX + COLS, :] = turned[0:COLS, :]
    turned[WIDE - COLS : WIDE, :] = turned[NX - COLS : NX, :]


def every(turned, col):
    return turned[pl.ds(col, LANES, stride=COLS), :]


def kernel(
    tiles,
    tracer,
    air,
    zonal,
    merid,
    substeps,
    out,
    mass_out,
    swept,
    turned,
    turned_more,
    back_turned,
    mine,
    mine_more,
    gathered,
    gathered_more,
    levels,
    levels_more,
    field,
    coef,
    last_mass,
    raw,
    rests,
    got_rests,
    dense,
    got_dense,
    outer,
    inner,
    kept_flux,
    kept_slope,
    edge_outer,
    edge_inner,
    got_outer,
    got_inner,
    faces,
    cells,
    masses_new,
    load_sem,
    gather_send,
    gather_recv,
    more_send,
    more_recv,
    outer_send,
    outer_recv,
    inner_send,
    inner_recv,
    edge_send,
    edge_recv,
):
    tile = lax.axis_index("tile")
    spec = lax.axis_index("spec")
    species = tracer.shape[0]
    groups = species // GROUP
    packs = species // PACK
    odd = lax.rem(tile, 2)
    is_odd = odd == 1
    outer_tile = tile + 2 * odd - 1
    inner_tile = tile + 1 - 2 * odd
    has_outer = jnp.logical_and(tile > 0, tile < tiles - 1)

    def place(row):
        return row + odd * (ROWS - 1 - 2 * row)

    def load(pack, row):
        part = pl.ds(pack * PACK, PACK)
        return pltpu.make_async_copy(
            tracer.at[part, row], out.at[part, row], load_sem.at[pack * ROWS + row]
        )

    def start_load(index, carry):
        load(lax.rem(index, packs), place(index // packs)).start()
        return carry

    lax.fori_loop(0, packs * ROWS, start_load, 0)

    half = LEVELS // 2
    partner = lax.rem(spec + half, LEVELS)
    side = (spec // half) * half
    peers = [side + lax.rem(spec + step, half) for step in range(1, half)]

    barrier = pltpu.get_barrier_semaphore()
    for peer in [partner] + peers:
        pl.semaphore_signal(barrier, inc=1, device_id=(tile, peer), device_id_type=MESH)
    pl.semaphore_signal(barrier, inc=1, device_id=(inner_tile, spec), device_id_type=MESH)

    @pl.when(has_outer)
    def _():
        pl.semaphore_signal(barrier, inc=1, device_id=(outer_tile, spec), device_id_type=MESH)

    mine[2 * ROWS :, :] = jnp.zeros((FIRST_ROWS - 2 * ROWS, NX), jnp.float32)
    mine_more[ROWS:, :] = jnp.zeros((LEVELS - ROWS, NX), jnp.float32)
    for row in range(ROWS):
        mine[row : row + 1, :] = air[place(row)]
        mine[ROWS + row : ROWS + row + 1, :] = zonal[place(row)]
        mine_more[row : row + 1, :] = merid[place(row)]
    gathered[spec] = mine[...]
    gathered_more[spec] = mine_more[...]

    greeted = half + 1 + has_outer.astype(jnp.int32)
    pl.semaphore_wait(barrier, greeted)

    first_kind = (mine, gathered, gather_send, gather_recv)
    more_kind = (mine_more, gathered_more, more_send, more_recv)

    def give(kind, level, peer, slot, source=None):
        own, target, send, recv = kind
        return pltpu.make_async_remote_copy(
            src_ref=own if source is None else source,
            dst_ref=target.at[level],
            send_sem=send.at[slot],
            recv_sem=recv.at[level],
            device_id=(tile, peer),
            device_id_type=MESH,
        )

    def give_own(kind):
        give(kind, spec, partner, 0).start()
        for k, peer in enumerate(peers):
            give(kind, spec, peer, 1 + k).start()

    def pass_on(kind):
        give(kind, partner, partner, 0).wait()
        for k, peer in enumerate(peers):
            give(kind, partner, peer, half + k, kind[1].at[partner]).start()

    def settle(kind):
        for k, peer in enumerate(peers):
            give(kind, spec, peer, 1 + k).wait_send()
            give(kind, partner, peer, half + k, kind[1].at[partner]).wait_send()
        for step in range(1, half):
            level = side + lax.rem(spec + half - step, half)
            for got in (level, lax.rem(level + half, LEVELS)):
                give(kind, got, partner, 0).wait_recv()

    def across(piece, swept_already):
        part = pl.ds(piece * PIECE, PIECE)
        if swept_already:
            source, target = dense.at[piece - RAW_PIECES], got_dense.at[piece - RAW_PIECES]
        else:
            lanes = pl.ds(0, WHOLE)
            source = out.at[part, pl.ds(odd * (ROWS - 2), 2), :, lanes]
            target = raw.at[part]
        return pltpu.make_async_remote_copy(
            src_ref=source,
            dst_ref=target,
            send_sem=outer_send.at[piece],
            recv_sem=outer_recv.at[piece],
            device_id=(outer_tile, spec),
            device_id_type=MESH,
        )

    def rest_across():
        return pltpu.make_async_remote_copy(
            src_ref=rests,
            dst_ref=got_rests,
            send_sem=edge_send.at[2],
            recv_sem=edge_recv.at[2],
            device_id=(outer_tile, spec),
            device_id_type=MESH,
        )

    lane = lax.broadcasted_iota(jnp.int32, (LEVELS, LANES), 1)

    def spot(index):
        return index // (2 * COLS), (index // COLS) % 2, index % COLS

    def pack_piece(piece):
        for index in range(DENSE):
            k, row, col = spot(index)
            value = swept[piece * PIECE + k, row, col]
            k, row, col = spot(DENSE + index // SLOTS)
            moved = pltpu.roll(
                swept[piece * PIECE + k, row, col], USED - SPARE * (index % SLOTS), 1
            )
            dense[piece - RAW_PIECES, index] = jnp.where(lane < USED, value, moved)

    def unpack_piece(piece):
        for index in range(DENSE):
            k, row, col = spot(index)
            outer[piece * PIECE + k, row, col] = got_dense[piece - RAW_PIECES, index]
        for last in range(ROW_SETS * COLS - DENSE):
            value = got_dense[piece - RAW_PIECES, last * SLOTS + SLOTS - 1]
            value = pltpu.roll(value, SPARE * (SLOTS - 1) + LANES - USED, 1)
            for slot in range(SLOTS - 1):
                moved = pltpu.roll(
                    got_dense[piece - RAW_PIECES, last * SLOTS + slot],
                    SPARE * slot + LANES - USED,
                    1,
                )
                inside = jnp.logical_and(lane >= SPARE * slot, lane < SPARE * (slot + 1))
                value = jnp.where(inside, moved, value)
            k, row, col = spot(DENSE + last)
            outer[piece * PIECE + k, row, col] = value

    def send_across(piece, swept_already, due=True):
        @pl.when(jnp.logical_and(has_outer, due))
        def _():
            if swept_already:
                pack_piece(piece)
            across(piece, swept_already).start()

    give_own(first_kind)
    for row in range(2):
        for pack in range(packs):
            load(pack, place(row)).wait()

    for group in range(RAW_GROUPS):
        for row in range(2):
            for k in range(GROUP // SHARE):
                rests[group, row, k] = jnp.concatenate(
                    [
                        out[
                            group * GROUP + j * (GROUP // SHARE) + k,
                            odd * (ROWS - 2) + row,
                            :,
                            WHOLE:NX,
                        ]
                        for j in range(SHARE)
                    ],
                    axis=1,
                )

    give_own(more_kind)
    for piece in range(1):
        send_across(piece, False)
    pass_on(first_kind)
    pass_on(more_kind)

    for piece in range(1, 3):
        send_across(piece, False)
    pl.when(has_outer)(lambda: rest_across().start())

    for buffer in (turned, turned_more):
        buffer[NX:WIDE, :] = jnp.ones((WIDE - NX, LANES), jnp.float32)

    def turn_in(read, write, count, rest=None):
        wide = count * LEVELS
        for col in range(COLS if rest is None else FULL):
            lanes = slice(col * LANES, min((col + 1) * LANES, NX))
            width = lanes.stop - lanes.start
            turned[lanes, 0:wide] = read(lanes).reshape(wide, width).T
        if rest is not None:
            few = wide // SHARE
            block = rest.reshape(few, LANES).T
            for j in range(SHARE):
                turned[WHOLE:NX, j * few : (j + 1) * few] = block[j * REST : (j + 1) * REST]
        wrap(turned)
        for col in range(COLS):
            write(col, every(turned, col).T[:wide].reshape(count, LEVELS, LANES))

    def turn_own(pack, row):
        part = pl.ds(pack * PACK, PACK)

        @pl.when(row >= 2)
        def _():
            load(pack, place(row)).wait()


        def write(col, value):
            swept[part, row, col] = value

        turn_in(lambda lanes: out[part, place(row), :, lanes], write, PACK)

    def turn_one(index, carry):
        send_across(3, False, index == packs * ROWS - 2)
        turn_own(index // ROWS, lax.rem(index, ROWS))
        return carry

    lax.fori_loop(0, packs * ROWS, turn_one, 0)
    settle(first_kind)

    def turn_fields(source, level_ref, rows):
        wide = LEVELS * rows
        for col in range(COLS):
            lanes = slice(col * LANES, min((col + 1) * LANES, NX))
            width = lanes.stop - lanes.start
            turned_more[lanes, 0:wide] = source[:, :, lanes].reshape(wide, width).T
        wrap(turned_more)
        for col in range(COLS):
            level_ref[col] = every(turned_more, col).T[:wide]

    turn_fields(gathered, levels, FIRST_ROWS)
    for col in range(COLS):
        for index in range(2):
            for row in range(ROWS):
                field[index, row, col] = levels[
                    col, pl.ds(index * ROWS + row, LEVELS, stride=FIRST_ROWS), :
                ]

    first = tile * ROWS

    def prepare(slot, place_of, mass, share):
        count = substeps[place_of]
        share = share / count.astype(jnp.float32)
        for step in range(STEPS):
            flux = jnp.where(step < count, share, 0.0)
            coef[slot, step, 0] = flux
            coef[slot, step, 1] = jnp.where(flux > 0, 1.0 - flux / west(mass), -1.0 - flux / mass)
            coef[slot, step, 2] = mass
            mass = mass + flux - east(flux)
            coef[slot, step, 3] = 1.0 / mass
        last_mass[slot] = mass

    def prepare_own(row, carry):
        prepare(row, first + place(row), field[0, row], field[1, row])
        return carry

    lax.fori_loop(0, ROWS, prepare_own, 0)

    def sweep(ref, group, row, slot):
        for k in range(GROUP):
            index = group * GROUP + k
            ratio = ref[index, row]
            for step in range(STEPS):
                flux = coef[slot, step, 0]
                fore = east(ratio) - ratio
                slope = half_slope(west(fore), fore)
                eastward = flux > 0
                value = jnp.where(eastward, west(ratio), ratio) + coef[slot, step, 1] * jnp.where(
                    eastward, west(slope), slope
                )
                carried = flux * value
                ratio = (coef[slot, step, 2] * ratio + carried - east(carried)) * coef[
                    slot, step, 3
                ]
            ref[index, row] = ratio

    def beside(group):
        part = pl.ds(group * GROUP, GROUP)
        return pltpu.make_async_remote_copy(
            src_ref=swept.at[part, pl.ds(ROWS - 2, 2)],
            dst_ref=inner.at[part],
            send_sem=inner_send.at[group],
            recv_sem=inner_recv.at[group],
            device_id=(inner_tile, spec),
            device_id_type=MESH,
        )

    send_across(4, False)

    def sweep_early(index, carry):
        row = lax.rem(index, 2)
        sweep(swept, RAW_GROUPS + index // 2, row, row)
        return carry

    lax.fori_loop(0, 2 * (groups - RAW_GROUPS), sweep_early, 0)

    def sweep_inner(group, carry):
        send_across(5 + group // 2, False, lax.rem(group, 2) == 0)

        def one(row, inside):
            sweep(swept, group, ROWS - 2 + row, ROWS - 2 + row)
            return inside

        lax.fori_loop(0, 2, one, 0)
        beside(group).start()
        return carry

    lax.fori_loop(0, groups, sweep_inner, 0)

    settle(more_kind)
    turn_fields(gathered_more, levels_more, LEVELS)
    for col in range(COLS):
        for row in range(ROWS):
            field[2, row, col] = levels_more[col, pl.ds(row, LEVELS, stride=LEVELS), :]

    for index in range(2):
        for row in range(2):
            edge_outer[2 * index + row] = field[index, row]
    edge_outer[4] = field[2, 0]
    edge_inner[0] = last_mass[ROWS - 1]
    edge_inner[1] = field[2, ROWS - 1]

    def edge(index):
        return pltpu.make_async_remote_copy(
            src_ref=(edge_outer, edge_inner)[index],
            dst_ref=(got_outer, got_inner)[index],
            send_sem=edge_send.at[index],
            recv_sem=edge_recv.at[index],
            device_id=((outer_tile, inner_tile)[index], spec),
            device_id_type=MESH,
        )

    edge(1).start()
    pl.when(has_outer)(lambda: edge(0).start())

    send_across(7, False)

    def sweep_middle(index, carry):
        send_across(RAW_PIECES + index // 4, True, lax.rem(index, 4) == 0)
        row = 2 + index // groups
        sweep(swept, lax.rem(index, groups), row, row)
        return carry

    lax.fori_loop(0, groups * (ROWS - 4), sweep_middle, 0)

    def sweep_late(index, carry):
        row = lax.rem(index, 2)
        sweep(swept, index // 2, row, row)
        return carry

    lax.fori_loop(0, 2 * RAW_GROUPS, sweep_late, 0)

    edge(1).wait()

    def row_mass(row):
        if row < 0:
            return last_mass[ROWS]
        return last_mass[row] if row < ROWS else got_inner[0]

    def own_flux(row):
        if row < 0:
            return got_outer[4]
        return field[2, row] if row < ROWS else got_inner[1]

    def make_face(face):
        flux = jnp.where(is_odd, -own_flux(face - 1), own_flux(face))
        if face == 0:
            flux = jnp.where(has_outer, flux, 0.0)
        faces[face, 0] = flux
        faces[face, 1] = jnp.where(
            flux > 0, 1.0 - flux / row_mass(face - 1), -1.0 - flux / row_mass(face)
        )

    def make_cell(row):
        mass = row_mass(row) + faces[row, 0] - faces[row + 1, 0]
        cells[row, 0] = row_mass(row)
        cells[row, 1] = 1.0 / mass
        masses_new[row] = mass

    for face in range(1, ROWS + 1):
        make_face(face)
    for row in range(1, ROWS):
        make_cell(row)
    masses_new[ROWS:] = jnp.zeros((PACK - ROWS, COLS, LEVELS, LANES), jnp.float32)

    def turn_out(read, write, count):
        wide = count * LEVELS
        for col in range(COLS):
            back_turned[pl.ds(col, LANES, stride=COLS), 0:wide] = read(col).reshape(wide, LANES).T
        for col in range(COLS):
            lanes = slice(col * LANES, min((col + 1) * LANES, NX))
            width = lanes.stop - lanes.start
            write(lanes, back_turned[lanes, :].T[:wide].reshape(count, LEVELS, width))

    def write_mass(lanes, value):
        for row in range(ROWS):
            mass_out[place(row), :, lanes] = value[row]

    def through(face, col, near, far, near_slope, far_slope):
        flux = faces[face, 0, col]
        onward = flux > 0
        value = jnp.where(onward, near, far) + faces[face, 1, col] * jnp.where(
            onward, near_slope, far_slope
        )
        return flux * value

    def renewed(row, col, ratio, enters, leaves):
        return (cells[row, 0, col] * ratio + enters - leaves) * cells[row, 1, col]

    def merid_far(index, col):
        rows = [swept[index, row, col] for row in range(ROWS)]
        rows += [inner[index, 1, col], inner[index, 0, col]]
        diffs = [rows[j + 1] - rows[j] for j in range(ROWS + 1)]
        slopes = [None] + [half_slope(diffs[j - 1], diffs[j]) for j in range(1, ROWS + 1)]
        carried = {
            face: through(
                face, col, rows[face - 1], rows[face], slopes[face - 1], slopes[face]
            )
            for face in range(2, ROWS + 1)
        }
        kept_flux[index, col] = carried[2]
        kept_slope[index, col] = slopes[1]
        for row in range(2, ROWS):
            swept[index, row, col] = renewed(row, col, rows[row], carried[row], carried[row + 1])

    def merid_near(index, col):
        rows = [outer[index, 1, col], outer[index, 0, col]]
        rows += [swept[index, row, col] for row in range(2)]
        diffs = [rows[j + 1] - rows[j] for j in range(3)]
        slopes = [half_slope(diffs[j], diffs[j + 1]) for j in range(2)]
        slopes.append(kept_slope[index, col])
        first_flux = through(0, col, rows[1], rows[2], slopes[0], slopes[1])
        second_flux = through(1, col, rows[2], rows[3], slopes[1], slopes[2])
        swept[index, 0, col] = renewed(0, col, rows[2], first_flux, second_flux)
        swept[index, 1, col] = renewed(1, col, rows[3], second_flux, kept_flux[index, col])

    def write_out(part, row):
        def write(lanes, value):
            out[part, place(row), :, lanes] = value

        return write

    def merid_all(group, work, pairs):
        def block(index, carry):
            col = lax.rem(index, COLS)
            for k in range(pairs):
                work(group * GROUP + (index // COLS) * pairs + k, col)
            return carry

        lax.fori_loop(0, COLS * (GROUP // pairs), block, 0)

    def far_group(group, carry):
        send_across(10 + group // 2, True, lax.rem(group, 2) == 0)
        beside(group).wait()
        merid_all(group, merid_far, 2)
        return carry

    lax.fori_loop(0, groups, far_group, 0)

    def far_out(index, carry):
        send_across(12 + index // 4, True, lax.rem(index, 4) == 0)
        part = pl.ds((index // (ROWS - 2)) * PACK, PACK)
        row = 2 + lax.rem(index, ROWS - 2)
        turn_out(lambda col: swept[part, row, col], write_out(part, row), PACK)
        return carry

    lax.fori_loop(0, packs * (ROWS - 2), far_out, 0)
    for piece in (14, 15):
        send_across(piece, True)


    @pl.when(has_outer)
    def _():
        edge(0).wait()
        rest_across().wait()

    @pl.when(jnp.logical_not(has_outer))
    def _():
        for row in range(2):
            got_outer[row] = field[0, row]
            got_outer[2 + row] = field[1, row]
        got_outer[4] = jnp.zeros((COLS, LEVELS, LANES), jnp.float32)

    def prepare_outer(row, carry):
        there = first + (1 - odd) * (-1 - row) + odd * (ROWS + row)
        there = jnp.where(has_outer, there, first + place(0))
        prepare(ROWS + row, there, got_outer[row], got_outer[2 + row])
        return carry

    lax.fori_loop(0, 2, prepare_outer, 0)

    make_face(0)
    make_cell(0)
    turn_out(lambda col: masses_new[:, col], write_mass, PACK)

    def near_row(row):
        return odd * row + (1 - odd) * (1 - row)

    def near_piece(piece):
        def block(col, carry):
            for k in range(PIECE):
                merid_near(piece * PIECE + k, col)
            return carry

        lax.fori_loop(0, COLS, block, 0, unroll=2)

    def near_group(group, swept_already):
        part = pl.ds(group * GROUP, GROUP)

        @pl.when(has_outer)
        def _():
            def arrive(k, inside):
                across(group * EACH + k, swept_already).wait()
                if swept_already:
                    unpack_piece(group * EACH + k)
                    near_piece(group * EACH + k)
                return inside

            lax.fori_loop(0, EACH, arrive, 0)

            def one(row, inside):
                def write(col, value):
                    outer[part, row, col] = value

                turn_in(
                    lambda lanes: raw[part, near_row(row), :, lanes],
                    write,
                    GROUP,
                    got_rests[group, near_row(row)],
                )
                sweep(outer, group, row, ROWS + row)
                return inside

            if not swept_already:
                lax.fori_loop(0, 2, one, 0)

        @pl.when(jnp.logical_not(has_outer))
        def _():
            def same(k, inside):
                for row in range(2):
                    outer[group * GROUP + k, row] = swept[group * GROUP + k, 0]
                return inside

            lax.fori_loop(0, GROUP, same, 0)

        if swept_already:

            @pl.when(jnp.logical_not(has_outer))
            def _():
                merid_all(group, merid_near, 4)

        else:
            merid_all(group, merid_near, 4)

        def back(row, inside):
            turn_out(lambda col: swept[part, row, col], write_out(part, row), GROUP)
            return inside

        lax.fori_loop(0, 2, back, 0)

    def near_raw(group, carry):
        near_group(group, False)
        return carry

    def near_swept(group, carry):
        near_group(group, True)
        return carry

    lax.fori_loop(0, RAW_GROUPS, near_raw, 0)
    lax.fori_loop(RAW_GROUPS, groups, near_swept, 0)


def store(ratios, masses, out, mass_out, sems):
    each = ratios.shape[0] // COPIES
    copies = [pltpu.make_async_copy(masses, mass_out, sems.at[COPIES])]
    for k in range(COPIES):
        part = pl.ds(k * each, each)
        copies.append(pltpu.make_async_copy(ratios.at[part], out.at[part], sems.at[k]))
    for copy in copies:
        copy.start()
    for copy in copies:
        copy.wait()


def shards(tiles, tracer, air_mass, zonal_flux, meridional_flux, substeps):
    species = tracer.shape[0]
    groups = species // GROUP
    rows_first = [jnp.transpose(x, (1, 0, 2)) for x in (air_mass, zonal_flux, meridional_flux)]
    f32 = jnp.float32
    dma = pltpu.SemaphoreType.DMA

    def body(*refs):
        kernel(tiles, *refs)

    def rows(*lead):
        return pltpu.VMEM((*lead, COLS, LEVELS, LANES), f32)

    vmem = pl.BlockSpec(memory_space=pltpu.VMEM)
    ratios, masses = pl.pallas_call(
        body,
        out_shape=(
            pltpu.VMEM((species, ROWS, LEVELS, NX), f32),
            pltpu.VMEM((ROWS, LEVELS, NX), f32),
        ),
        in_specs=[
            pl.BlockSpec(memory_space=pl.ANY),
            vmem,
            vmem,
            vmem,
            pl.BlockSpec(memory_space=pltpu.SMEM),
        ],
        out_specs=(vmem, vmem),
        scratch_shapes=[
            rows(species, ROWS),
            pltpu.VMEM((WIDE, LANES), f32),
            pltpu.VMEM((WIDE, LANES), f32),
            pltpu.VMEM((WIDE, LANES), f32),
            pltpu.VMEM((FIRST_ROWS, NX), f32),
            pltpu.VMEM((LEVELS, NX), f32),
            pltpu.VMEM((LEVELS, FIRST_ROWS, NX), f32),
            pltpu.VMEM((LEVELS, LEVELS, NX), f32),
            pltpu.VMEM((COLS, LEVELS * FIRST_ROWS, LANES), f32),
            pltpu.VMEM((COLS, LEVELS * LEVELS, LANES), f32),
            rows(3, ROWS),
            rows(ROWS + 2, STEPS, 4),
            rows(ROWS + 2),
            pltpu.VMEM((RAW_GROUPS * GROUP, 2, LEVELS, WHOLE), f32),
            pltpu.VMEM((RAW_GROUPS, 2, GROUP // SHARE, LEVELS, LANES), f32),
            pltpu.VMEM((RAW_GROUPS, 2, GROUP // SHARE, LEVELS, LANES), f32),
            pltpu.VMEM((species // PIECE - RAW_PIECES, DENSE, LEVELS, LANES), f32),
            pltpu.VMEM((species // PIECE - RAW_PIECES, DENSE, LEVELS, LANES), f32),
            rows(species, 2),
            rows(species, 2),
            rows(species),
            rows(species),
            rows(5),
            rows(2),
            rows(5),
            rows(2),
            rows(ROWS + 1, 2),
            rows(ROWS, 2),
            rows(PACK),
            dma((species // PACK * ROWS,)),
            dma((LEVELS,)),
            dma((LEVELS,)),
            dma((LEVELS,)),
            dma((LEVELS,)),
            dma((species // PIECE,)),
            dma((species // PIECE,)),
            dma((groups,)),
            dma((groups,)),
            dma((3,)),
            dma((3,)),
        ],
        compiler_params=pltpu.CompilerParams(
            collective_id=0, has_side_effects=True, vmem_limit_bytes=50 * 2**20
        ),
        cost_estimate=pl.CostEstimate(flops=10**9, bytes_accessed=2 * 10**7, transcendentals=0),
    )(jnp.transpose(tracer, (0, 2, 1, 3)), *rows_first, substeps)
    ratios, masses = pl.pallas_call(
        store,
        out_shape=(
            jax.ShapeDtypeStruct((species, ROWS, LEVELS, NX), f32),
            jax.ShapeDtypeStruct((ROWS, LEVELS, NX), f32),
        ),
        in_specs=[vmem, vmem],
        out_specs=(pl.BlockSpec(memory_space=pl.ANY), pl.BlockSpec(memory_space=pl.ANY)),
        scratch_shapes=[dma((COPIES + 1,))],
        compiler_params=pltpu.CompilerParams(vmem_limit_bytes=16 * 2**20),
    )(ratios, masses)
    return jnp.transpose(ratios, (0, 2, 1, 3)), jnp.transpose(masses, (1, 0, 2))


def solution(mesh):
    tiles = mesh.shape["tile"]

    def run(*args):
        return shards(tiles, *args)

    placed = (
        P("spec", None, "tile", None),
        P("spec", "tile", None),
        P("spec", "tile", None),
        P("spec", "tile", None),
        P(),
    )
    return jax.shard_map(
        run,
        mesh=mesh,
        in_specs=placed,
        out_specs=(P("spec", None, "tile", None), P(None, "tile", None)),
        check_vma=False,
    )
```

```python
import jax
import jax.numpy as jnp
from jax import lax
from jax.experimental import pallas as pl
from jax.experimental.pallas import tpu as pltpu
from jax.sharding import PartitionSpec as P

MESH = pl.DeviceIdType.MESH
NX = 1440
LANES = 128
COLS = 12
WIDE = COLS * LANES
LEVELS = 8
ROWS = 6
STEPS = 4
GROUP = 8
PIECE = 2
EACH = GROUP // PIECE
RAW_GROUPS = 2
RAW_PIECES = RAW_GROUPS * EACH
WHOLE = NX // LANES * LANES
REST = NX - WHOLE
SHARE = LANES // REST
USED = NX // COLS
SPARE = LANES - USED
SLOTS = USED // SPARE
COPIES = 4
ROW_SETS = PIECE * 2
DENSE = ROW_SETS * COLS * USED // LANES
PACK = LANES // LEVELS
FIRST_ROWS = 16
FULL = NX // LANES


def east(value):
    return jnp.concatenate([value[1:], pltpu.roll(value[0], LANES - 1, 1)[None]], axis=0)


def west(value):
    return jnp.concatenate([pltpu.roll(value[COLS - 1], 1, 1)[None], value[: COLS - 1]], axis=0)


def half_slope(back, fore):
    low = jnp.maximum(jnp.minimum(back, fore), 0.0)
    high = jnp.minimum(jnp.maximum(back, fore), 0.0)
    return jnp.maximum(jnp.minimum(0.25 * (back + fore), low), high)


def wrap(turned):
    turned[NX : NX + COLS, :] = turned[0:COLS, :]
    turned[WIDE - COLS : WIDE, :] = turned[NX - COLS : NX, :]


def every(turned, col):
    return turned[pl.ds(col, LANES, stride=COLS), :]


def kernel(
    tiles,
    tracer,
    air,
    zonal,
    merid,
    substeps,
    out,
    mass_out,
    swept,
    turned,
    turned_more,
    back_turned,
    mine,
    mine_more,
    gathered,
    gathered_more,
    levels,
    levels_more,
    field,
    coef,
    last_mass,
    raw,
    rests,
    got_rests,
    dense,
    got_dense,
    outer,
    inner,
    kept_flux,
    kept_slope,
    edge_outer,
    edge_inner,
    got_outer,
    got_inner,
    faces,
    cells,
    masses_new,
    load_sem,
    gather_send,
    gather_recv,
    more_send,
    more_recv,
    outer_send,
    outer_recv,
    inner_send,
    inner_recv,
    edge_send,
    edge_recv,
):
    tile = lax.axis_index("tile")
    spec = lax.axis_index("spec")
    species = tracer.shape[0]
    groups = species // GROUP
    packs = species // PACK
    odd = lax.rem(tile, 2)
    is_odd = odd == 1
    outer_tile = tile + 2 * odd - 1
    inner_tile = tile + 1 - 2 * odd
    has_outer = jnp.logical_and(tile > 0, tile < tiles - 1)

    def place(row):
        return row + odd * (ROWS - 1 - 2 * row)

    def load(pack, row):
        part = pl.ds(pack * PACK, PACK)
        return pltpu.make_async_copy(
            tracer.at[part, row], out.at[part, row], load_sem.at[pack * ROWS + row]
        )

    def start_load(index, carry):
        load(lax.rem(index, packs), place(index // packs)).start()
        return carry

    lax.fori_loop(0, packs * ROWS, start_load, 0)

    half = LEVELS // 2
    partner = lax.rem(spec + half, LEVELS)
    side = (spec // half) * half
    peers = [side + lax.rem(spec + step, half) for step in range(1, half)]

    barrier = pltpu.get_barrier_semaphore()
    for peer in [partner] + peers:
        pl.semaphore_signal(barrier, inc=1, device_id=(tile, peer), device_id_type=MESH)
    pl.semaphore_signal(barrier, inc=1, device_id=(inner_tile, spec), device_id_type=MESH)

    @pl.when(has_outer)
    def _():
        pl.semaphore_signal(barrier, inc=1, device_id=(outer_tile, spec), device_id_type=MESH)

    mine[2 * ROWS :, :] = jnp.zeros((FIRST_ROWS - 2 * ROWS, NX), jnp.float32)
    mine_more[ROWS:, :] = jnp.zeros((LEVELS - ROWS, NX), jnp.float32)
    for row in range(ROWS):
        mine[row : row + 1, :] = air[place(row)]
        mine[ROWS + row : ROWS + row + 1, :] = zonal[place(row)]
        mine_more[row : row + 1, :] = merid[place(row)]
    gathered[spec] = mine[...]
    gathered_more[spec] = mine_more[...]

    greeted = half + 1 + has_outer.astype(jnp.int32)
    pl.semaphore_wait(barrier, greeted)

    first_kind = (mine, gathered, gather_send, gather_recv)
    more_kind = (mine_more, gathered_more, more_send, more_recv)

    def give(kind, level, peer, slot, source=None):
        own, target, send, recv = kind
        return pltpu.make_async_remote_copy(
            src_ref=own if source is None else source,
            dst_ref=target.at[level],
            send_sem=send.at[slot],
            recv_sem=recv.at[level],
            device_id=(tile, peer),
            device_id_type=MESH,
        )

    def give_own(kind):
        give(kind, spec, partner, 0).start()
        for k, peer in enumerate(peers):
            give(kind, spec, peer, 1 + k).start()

    def pass_on(kind):
        give(kind, partner, partner, 0).wait()
        for k, peer in enumerate(peers):
            give(kind, partner, peer, half + k, kind[1].at[partner]).start()

    def settle(kind):
        for k, peer in enumerate(peers):
            give(kind, spec, peer, 1 + k).wait_send()
            give(kind, partner, peer, half + k, kind[1].at[partner]).wait_send()
        for step in range(1, half):
            level = side + lax.rem(spec + half - step, half)
            for got in (level, lax.rem(level + half, LEVELS)):
                give(kind, got, partner, 0).wait_recv()

    def across(piece, swept_already):
        part = pl.ds(piece * PIECE, PIECE)
        if swept_already:
            source, target = dense.at[piece - RAW_PIECES], got_dense.at[piece - RAW_PIECES]
        else:
            lanes = pl.ds(0, WHOLE)
            source = out.at[part, pl.ds(odd * (ROWS - 2), 2), :, lanes]
            target = raw.at[part]
        return pltpu.make_async_remote_copy(
            src_ref=source,
            dst_ref=target,
            send_sem=outer_send.at[piece],
            recv_sem=outer_recv.at[piece],
            device_id=(outer_tile, spec),
            device_id_type=MESH,
        )

    def rest_across():
        return pltpu.make_async_remote_copy(
            src_ref=rests,
            dst_ref=got_rests,
            send_sem=edge_send.at[2],
            recv_sem=edge_recv.at[2],
            device_id=(outer_tile, spec),
            device_id_type=MESH,
        )

    lane = lax.broadcasted_iota(jnp.int32, (LEVELS, LANES), 1)

    def spot(index):
        return index // (2 * COLS), (index // COLS) % 2, index % COLS

    def pack_piece(piece):
        for index in range(DENSE):
            k, row, col = spot(index)
            value = swept[piece * PIECE + k, row, col]
            k, row, col = spot(DENSE + index // SLOTS)
            moved = pltpu.roll(
                swept[piece * PIECE + k, row, col], USED - SPARE * (index % SLOTS), 1
            )
            dense[piece - RAW_PIECES, index] = jnp.where(lane < USED, value, moved)

    def unpack_piece(piece):
        for index in range(DENSE):
            k, row, col = spot(index)
            outer[piece * PIECE + k, row, col] = got_dense[piece - RAW_PIECES, index]
        for last in range(ROW_SETS * COLS - DENSE):
            value = got_dense[piece - RAW_PIECES, last * SLOTS + SLOTS - 1]
            value = pltpu.roll(value, SPARE * (SLOTS - 1) + LANES - USED, 1)
            for slot in range(SLOTS - 1):
                moved = pltpu.roll(
                    got_dense[piece - RAW_PIECES, last * SLOTS + slot],
                    SPARE * slot + LANES - USED,
                    1,
                )
                inside = jnp.logical_and(lane >= SPARE * slot, lane < SPARE * (slot + 1))
                value = jnp.where(inside, moved, value)
            k, row, col = spot(DENSE + last)
            outer[piece * PIECE + k, row, col] = value

    def send_across(piece, swept_already, due=True):
        @pl.when(jnp.logical_and(has_outer, due))
        def _():
            if swept_already:
                pack_piece(piece)
            across(piece, swept_already).start()

    give_own(first_kind)
    for row in range(2):
        for pack in range(packs):
            load(pack, place(row)).wait()

    for group in range(RAW_GROUPS):
        for row in range(2):
            for k in range(GROUP // SHARE):
                rests[group, row, k] = jnp.concatenate(
                    [
                        out[
                            group * GROUP + j * (GROUP // SHARE) + k,
                            odd * (ROWS - 2) + row,
                            :,
                            WHOLE:NX,
                        ]
                        for j in range(SHARE)
                    ],
                    axis=1,
                )

    send_across(0, False)
    pass_on(first_kind)
    send_across(1, False)
    send_across(2, False)
    give_own(more_kind)
    pl.when(has_outer)(lambda: rest_across().start())

    for buffer in (turned, turned_more):
        buffer[NX:WIDE, :] = jnp.ones((WIDE - NX, LANES), jnp.float32)

    def turn_in(read, write, count, rest=None):
        wide = count * LEVELS
        for col in range(COLS if rest is None else FULL):
            lanes = slice(col * LANES, min((col + 1) * LANES, NX))
            width = lanes.stop - lanes.start
            turned[lanes, 0:wide] = read(lanes).reshape(wide, width).T
        if rest is not None:
            few = wide // SHARE
            block = rest.reshape(few, LANES).T
            for j in range(SHARE):
                turned[WHOLE:NX, j * few : (j + 1) * few] = block[j * REST : (j + 1) * REST]
        wrap(turned)
        for col in range(COLS):
            write(col, every(turned, col).T[:wide].reshape(count, LEVELS, LANES))

    def turn_own(pack, row):
        part = pl.ds(pack * PACK, PACK)

        @pl.when(row >= 2)
        def _():
            load(pack, place(row)).wait()


        def write(col, value):
            swept[part, row, col] = value

        turn_in(lambda lanes: out[part, place(row), :, lanes], write, PACK)

    def turn_one(index, carry):
        send_across(3, False, index == packs * ROWS - 2)
        turn_own(index // ROWS, lax.rem(index, ROWS))
        return carry

    lax.fori_loop(0, packs * ROWS, turn_one, 0)
    pass_on(more_kind)
    settle(first_kind)

    def turn_fields(source, level_ref, rows):
        wide = LEVELS * rows
        for col in range(COLS):
            lanes = slice(col * LANES, min((col + 1) * LANES, NX))
            width = lanes.stop - lanes.start
            turned_more[lanes, 0:wide] = source[:, :, lanes].reshape(wide, width).T
        wrap(turned_more)
        for col in range(COLS):
            level_ref[col] = every(turned_more, col).T[:wide]

    turn_fields(gathered, levels, FIRST_ROWS)
    for col in range(COLS):
        for index in range(2):
            for row in range(ROWS):
                field[index, row, col] = levels[
                    col, pl.ds(index * ROWS + row, LEVELS, stride=FIRST_ROWS), :
                ]

    first = tile * ROWS

    def prepare(slot, place_of, mass, share):
        count = substeps[place_of]
        share = share / count.astype(jnp.float32)
        for step in range(STEPS):
            flux = jnp.where(step < count, share, 0.0)
            coef[slot, step, 0] = flux
            coef[slot, step, 1] = jnp.where(flux > 0, 1.0 - flux / west(mass), -1.0 - flux / mass)
            coef[slot, step, 2] = mass
            mass = mass + flux - east(flux)
            coef[slot, step, 3] = 1.0 / mass
        last_mass[slot] = mass

    def prepare_own(row, carry):
        prepare(row, first + place(row), field[0, row], field[1, row])
        return carry

    lax.fori_loop(0, ROWS, prepare_own, 0)

    def sweep(ref, group, row, slot):
        for k in range(GROUP):
            index = group * GROUP + k
            ratio = ref[index, row]
            for step in range(STEPS):
                flux = coef[slot, step, 0]
                fore = east(ratio) - ratio
                slope = half_slope(west(fore), fore)
                eastward = flux > 0
                value = jnp.where(eastward, west(ratio), ratio) + coef[slot, step, 1] * jnp.where(
                    eastward, west(slope), slope
                )
                carried = flux * value
                ratio = (coef[slot, step, 2] * ratio + carried - east(carried)) * coef[
                    slot, step, 3
                ]
            ref[index, row] = ratio

    def beside(group):
        part = pl.ds(group * GROUP, GROUP)
        return pltpu.make_async_remote_copy(
            src_ref=swept.at[part, pl.ds(ROWS - 2, 2)],
            dst_ref=inner.at[part],
            send_sem=inner_send.at[group],
            recv_sem=inner_recv.at[group],
            device_id=(inner_tile, spec),
            device_id_type=MESH,
        )

    send_across(4, False)

    def sweep_early(index, carry):
        row = lax.rem(index, 2)
        sweep(swept, RAW_GROUPS + index // 2, row, row)
        return carry

    lax.fori_loop(0, 2 * (groups - RAW_GROUPS), sweep_early, 0)

    def sweep_inner(group, carry):
        send_across(5 + group // 2, False, lax.rem(group, 2) == 0)

        def one(row, inside):
            sweep(swept, group, ROWS - 2 + row, ROWS - 2 + row)
            return inside

        lax.fori_loop(0, 2, one, 0)
        beside(group).start()
        return carry

    lax.fori_loop(0, groups, sweep_inner, 0)

    settle(more_kind)
    turn_fields(gathered_more, levels_more, LEVELS)
    for col in range(COLS):
        for row in range(ROWS):
            field[2, row, col] = levels_more[col, pl.ds(row, LEVELS, stride=LEVELS), :]

    for index in range(2):
        for row in range(2):
            edge_outer[2 * index + row] = field[index, row]
    edge_outer[4] = field[2, 0]
    edge_inner[0] = last_mass[ROWS - 1]
    edge_inner[1] = field[2, ROWS - 1]

    def edge(index):
        return pltpu.make_async_remote_copy(
            src_ref=(edge_outer, edge_inner)[index],
            dst_ref=(got_outer, got_inner)[index],
            send_sem=edge_send.at[index],
            recv_sem=edge_recv.at[index],
            device_id=((outer_tile, inner_tile)[index], spec),
            device_id_type=MESH,
        )

    edge(1).start()
    pl.when(has_outer)(lambda: edge(0).start())

    send_across(7, False)

    def sweep_middle(index, carry):
        send_across(RAW_PIECES + index // 4, True, lax.rem(index, 4) == 0)
        row = 2 + index // groups
        sweep(swept, lax.rem(index, groups), row, row)
        return carry

    lax.fori_loop(0, groups * (ROWS - 4), sweep_middle, 0)

    def sweep_late(index, carry):
        row = lax.rem(index, 2)
        sweep(swept, index // 2, row, row)
        return carry

    lax.fori_loop(0, 2 * RAW_GROUPS, sweep_late, 0)

    edge(1).wait()

    def row_mass(row):
        if row < 0:
            return last_mass[ROWS]
        return last_mass[row] if row < ROWS else got_inner[0]

    def own_flux(row):
        if row < 0:
            return got_outer[4]
        return field[2, row] if row < ROWS else got_inner[1]

    def make_face(face):
        flux = jnp.where(is_odd, -own_flux(face - 1), own_flux(face))
        if face == 0:
            flux = jnp.where(has_outer, flux, 0.0)
        faces[face, 0] = flux
        faces[face, 1] = jnp.where(
            flux > 0, 1.0 - flux / row_mass(face - 1), -1.0 - flux / row_mass(face)
        )

    def make_cell(row):
        mass = row_mass(row) + faces[row, 0] - faces[row + 1, 0]
        cells[row, 0] = row_mass(row)
        cells[row, 1] = 1.0 / mass
        masses_new[row] = mass

    for face in range(1, ROWS + 1):
        make_face(face)
    for row in range(1, ROWS):
        make_cell(row)
    masses_new[ROWS:] = jnp.zeros((PACK - ROWS, COLS, LEVELS, LANES), jnp.float32)

    def turn_out(read, write, count):
        wide = count * LEVELS
        for col in range(COLS):
            back_turned[pl.ds(col, LANES, stride=COLS), 0:wide] = read(col).reshape(wide, LANES).T
        for col in range(COLS):
            lanes = slice(col * LANES, min((col + 1) * LANES, NX))
            width = lanes.stop - lanes.start
            write(lanes, back_turned[lanes, :].T[:wide].reshape(count, LEVELS, width))

    def write_mass(lanes, value):
        for row in range(ROWS):
            mass_out[place(row), :, lanes] = value[row]

    def through(face, col, near, far, near_slope, far_slope):
        flux = faces[face, 0, col]
        onward = flux > 0
        value = jnp.where(onward, near, far) + faces[face, 1, col] * jnp.where(
            onward, near_slope, far_slope
        )
        return flux * value

    def renewed(row, col, ratio, enters, leaves):
        return (cells[row, 0, col] * ratio + enters - leaves) * cells[row, 1, col]

    def merid_far(index, col):
        rows = [swept[index, row, col] for row in range(ROWS)]
        rows += [inner[index, 1, col], inner[index, 0, col]]
        diffs = [rows[j + 1] - rows[j] for j in range(ROWS + 1)]
        slopes = [None] + [half_slope(diffs[j - 1], diffs[j]) for j in range(1, ROWS + 1)]
        carried = {
            face: through(
                face, col, rows[face - 1], rows[face], slopes[face - 1], slopes[face]
            )
            for face in range(2, ROWS + 1)
        }
        kept_flux[index, col] = carried[2]
        kept_slope[index, col] = slopes[1]
        for row in range(2, ROWS):
            swept[index, row, col] = renewed(row, col, rows[row], carried[row], carried[row + 1])

    def merid_near(index, col):
        rows = [outer[index, 1, col], outer[index, 0, col]]
        rows += [swept[index, row, col] for row in range(2)]
        diffs = [rows[j + 1] - rows[j] for j in range(3)]
        slopes = [half_slope(diffs[j], diffs[j + 1]) for j in range(2)]
        slopes.append(kept_slope[index, col])
        first_flux = through(0, col, rows[1], rows[2], slopes[0], slopes[1])
        second_flux = through(1, col, rows[2], rows[3], slopes[1], slopes[2])
        swept[index, 0, col] = renewed(0, col, rows[2], first_flux, second_flux)
        swept[index, 1, col] = renewed(1, col, rows[3], second_flux, kept_flux[index, col])

    def write_out(part, row):
        def write(lanes, value):
            out[part, place(row), :, lanes] = value

        return write

    def merid_all(group, work, pairs):
        def block(index, carry):
            col = lax.rem(index, COLS)
            for k in range(pairs):
                work(group * GROUP + (index // COLS) * pairs + k, col)
            return carry

        lax.fori_loop(0, COLS * (GROUP // pairs), block, 0)

    def far_group(group, carry):
        send_across(10 + group // 2, True, lax.rem(group, 2) == 0)
        beside(group).wait()
        merid_all(group, merid_far, 2)
        return carry

    lax.fori_loop(0, groups, far_group, 0)

    def far_out(index, carry):
        send_across(12 + index // 4, True, lax.rem(index, 4) == 0)
        part = pl.ds((index // (ROWS - 2)) * PACK, PACK)
        row = 2 + lax.rem(index, ROWS - 2)
        turn_out(lambda col: swept[part, row, col], write_out(part, row), PACK)
        return carry

    lax.fori_loop(0, packs * (ROWS - 2), far_out, 0)
    for piece in (14, 15):
        send_across(piece, True)


    @pl.when(has_outer)
    def _():
        edge(0).wait()
        rest_across().wait()

    @pl.when(jnp.logical_not(has_outer))
    def _():
        for row in range(2):
            got_outer[row] = field[0, row]
            got_outer[2 + row] = field[1, row]
        got_outer[4] = jnp.zeros((COLS, LEVELS, LANES), jnp.float32)

    def prepare_outer(row, carry):
        there = first + (1 - odd) * (-1 - row) + odd * (ROWS + row)
        there = jnp.where(has_outer, there, first + place(0))
        prepare(ROWS + row, there, got_outer[row], got_outer[2 + row])
        return carry

    lax.fori_loop(0, 2, prepare_outer, 0)

    make_face(0)
    make_cell(0)
    turn_out(lambda col: masses_new[:, col], write_mass, PACK)

    def near_row(row):
        return odd * row + (1 - odd) * (1 - row)

    def near_piece(piece):
        def block(col, carry):
            for k in range(PIECE):
                merid_near(piece * PIECE + k, col)
            return carry

        lax.fori_loop(0, COLS, block, 0, unroll=2)

    def near_group(group, swept_already):
        part = pl.ds(group * GROUP, GROUP)

        @pl.when(has_outer)
        def _():
            def arrive(k, inside):
                across(group * EACH + k, swept_already).wait()
                if swept_already:
                    unpack_piece(group * EACH + k)
                    near_piece(group * EACH + k)
                return inside

            lax.fori_loop(0, EACH, arrive, 0)

            def one(row, inside):
                def write(col, value):
                    outer[part, row, col] = value

                turn_in(
                    lambda lanes: raw[part, near_row(row), :, lanes],
                    write,
                    GROUP,
                    got_rests[group, near_row(row)],
                )
                sweep(outer, group, row, ROWS + row)
                return inside

            if not swept_already:
                lax.fori_loop(0, 2, one, 0)

        @pl.when(jnp.logical_not(has_outer))
        def _():
            def same(k, inside):
                for row in range(2):
                    outer[group * GROUP + k, row] = swept[group * GROUP + k, 0]
                return inside

            lax.fori_loop(0, GROUP, same, 0)

        if swept_already:

            @pl.when(jnp.logical_not(has_outer))
            def _():
                merid_all(group, merid_near, 4)

        else:
            merid_all(group, merid_near, 4)

        def back(row, inside):
            turn_out(lambda col: swept[part, row, col], write_out(part, row), GROUP)
            return inside

        lax.fori_loop(0, 2, back, 0)

    def near_raw(group, carry):
        near_group(group, False)
        return carry

    def near_swept(group, carry):
        near_group(group, True)
        return carry

    lax.fori_loop(0, RAW_GROUPS, near_raw, 0)
    lax.fori_loop(RAW_GROUPS, groups, near_swept, 0)


def store(ratios, masses, out, mass_out, sems):
    each = ratios.shape[0] // COPIES
    copies = [pltpu.make_async_copy(masses, mass_out, sems.at[COPIES])]
    for k in range(COPIES):
        part = pl.ds(k * each, each)
        copies.append(pltpu.make_async_copy(ratios.at[part], out.at[part], sems.at[k]))
    for copy in copies:
        copy.start()
    for copy in copies:
        copy.wait()


def shards(tiles, tracer, air_mass, zonal_flux, meridional_flux, substeps):
    species = tracer.shape[0]
    groups = species // GROUP
    rows_first = [jnp.transpose(x, (1, 0, 2)) for x in (air_mass, zonal_flux, meridional_flux)]
    f32 = jnp.float32
    dma = pltpu.SemaphoreType.DMA

    def body(*refs):
        kernel(tiles, *refs)

    def rows(*lead):
        return pltpu.VMEM((*lead, COLS, LEVELS, LANES), f32)

    vmem = pl.BlockSpec(memory_space=pltpu.VMEM)
    ratios, masses = pl.pallas_call(
        body,
        out_shape=(
            pltpu.VMEM((species, ROWS, LEVELS, NX), f32),
            pltpu.VMEM((ROWS, LEVELS, NX), f32),
        ),
        in_specs=[
            pl.BlockSpec(memory_space=pl.ANY),
            vmem,
            vmem,
            vmem,
            pl.BlockSpec(memory_space=pltpu.SMEM),
        ],
        out_specs=(vmem, vmem),
        scratch_shapes=[
            rows(species, ROWS),
            pltpu.VMEM((WIDE, LANES), f32),
            pltpu.VMEM((WIDE, LANES), f32),
            pltpu.VMEM((WIDE, LANES), f32),
            pltpu.VMEM((FIRST_ROWS, NX), f32),
            pltpu.VMEM((LEVELS, NX), f32),
            pltpu.VMEM((LEVELS, FIRST_ROWS, NX), f32),
            pltpu.VMEM((LEVELS, LEVELS, NX), f32),
            pltpu.VMEM((COLS, LEVELS * FIRST_ROWS, LANES), f32),
            pltpu.VMEM((COLS, LEVELS * LEVELS, LANES), f32),
            rows(3, ROWS),
            rows(ROWS + 2, STEPS, 4),
            rows(ROWS + 2),
            pltpu.VMEM((RAW_GROUPS * GROUP, 2, LEVELS, WHOLE), f32),
            pltpu.VMEM((RAW_GROUPS, 2, GROUP // SHARE, LEVELS, LANES), f32),
            pltpu.VMEM((RAW_GROUPS, 2, GROUP // SHARE, LEVELS, LANES), f32),
            pltpu.VMEM((species // PIECE - RAW_PIECES, DENSE, LEVELS, LANES), f32),
            pltpu.VMEM((species // PIECE - RAW_PIECES, DENSE, LEVELS, LANES), f32),
            rows(species, 2),
            rows(species, 2),
            rows(species),
            rows(species),
            rows(5),
            rows(2),
            rows(5),
            rows(2),
            rows(ROWS + 1, 2),
            rows(ROWS, 2),
            rows(PACK),
            dma((species // PACK * ROWS,)),
            dma((LEVELS,)),
            dma((LEVELS,)),
            dma((LEVELS,)),
            dma((LEVELS,)),
            dma((species // PIECE,)),
            dma((species // PIECE,)),
            dma((groups,)),
            dma((groups,)),
            dma((3,)),
            dma((3,)),
        ],
        compiler_params=pltpu.CompilerParams(
            collective_id=0, has_side_effects=True, vmem_limit_bytes=50 * 2**20
        ),
        cost_estimate=pl.CostEstimate(flops=10**9, bytes_accessed=2 * 10**7, transcendentals=0),
    )(jnp.transpose(tracer, (0, 2, 1, 3)), *rows_first, substeps)
    ratios, masses = pl.pallas_call(
        store,
        out_shape=(
            jax.ShapeDtypeStruct((species, ROWS, LEVELS, NX), f32),
            jax.ShapeDtypeStruct((ROWS, LEVELS, NX), f32),
        ),
        in_specs=[vmem, vmem],
        out_specs=(pl.BlockSpec(memory_space=pl.ANY), pl.BlockSpec(memory_space=pl.ANY)),
        scratch_shapes=[dma((COPIES + 1,))],
        compiler_params=pltpu.CompilerParams(vmem_limit_bytes=16 * 2**20),
    )(ratios, masses)
    return jnp.transpose(ratios, (0, 2, 1, 3)), jnp.transpose(masses, (1, 0, 2))


def solution(mesh):
    tiles = mesh.shape["tile"]

    def run(*args):
        return shards(tiles, *args)

    placed = (
        P("spec", None, "tile", None),
        P("spec", "tile", None),
        P("spec", "tile", None),
        P("spec", "tile", None),
        P(),
    )
    return jax.shard_map(
        run,
        mesh=mesh,
        in_specs=placed,
        out_specs=(P("spec", None, "tile", None), P(None, "tile", None)),
        check_vma=False,
    )
```
